512 devices in a mesh: leaf: 128 (over z, x, core), sub: 4 (over y).
Axes of the slice: x: 4, y: 4, z: 16, core: 2. Of those that a mesh axis runs over, the one named last changes fastest.
Arguments:
- positions: float32 [3, 32, 131072], P(None, None, ('leaf', 'sub')), may hold values from 0 to 2, as said below
- charges: float32 [32, 131072], P(None, ('leaf', 'sub')), may hold values from -1.6 to 1.6
- m2l_ops: float32 [216, 3456], replicated, may hold values from -3 to 3
- near_list: int32 [131072, 27], P(('leaf', 'sub')), may hold values from -1 to 2047, as said below
- far_list: int32 [131072, 16], P(('leaf', 'sub')), may hold values from -1 to 2047, as said below
- send_slots: int32 [512, 128, 8], P(('leaf', 'sub')), may hold values from -1 to 255, as said below
Outputs:
- potential: float32 [32, 131072], P(None, ('leaf', 'sub'))
The draws below stay inside these ranges and needn't reach their ends.
Inputs may be any that keep to these rules, and one draw needn't show every extreme that they name: `positions`: all 32 bodies of a leaf lie in one unit cube with integer corners, at least 0.01 inside its faces; leaves follow their cubes' Morton order. send_slots[g, p, c] is a leaf of device g (counted among its own 256) that g sends to the device of index p along leaf with g's index along sub, or -1. In each block [g, p] the live entries come first and are distinct; the block to g's own index is empty; a block to an index next to g's holds at most 8 live entries and one such block of every device holds exactly 8; any other block holds 1 to 3 and one of every device holds exactly 3. Entry 0 of row i is leaf i itself, as a row column. Every entry e >= 1024 names a live slot of send_slots, and every live slot sent to a device is named by some near_list entry of its leaves. Every entry e >= 1024 names a live slot of send_slots, and every live slot sent to a device is named by some far_list entry of its leaves.
All inputs are finite; a program needn't handle non-finite values.
Results may differ from the reference program's by a relative error of at most 0.0003.
Values sent between devices are 32-bit elements; how exact they have to be, the bound alone decides.
A program may use at most 192 MiB of HBM per device.

```python
import math
import jax
import jax.numpy as jnp
from jax import lax

LEAF_DEV = 256
NB = 32
ORDER = 6
NODES = 216
NEAR = 27
FAR = 16
CAP = 8
CAP_FAR = 3
LEAVES = 131072
N_LEAF = 128
N_SUB = 4


def cell_corners(key):
    leaf_ids = jnp.arange(LEAVES, dtype=jnp.int32)
    bounds = jnp.sort(jax.random.randint(key, (7,), 0, LEAVES + 1))
    cube_index = jnp.sum((leaf_ids[:, None] >= bounds[None, :]).astype(jnp.int32), axis=1)
    corners = []
    for axis_id in range(3):
        corners.append(cube_index >> axis_id & 1)
    return jnp.stack(corners).astype(jnp.float32)


def plan_tables(key):
    devices = N_LEAF * N_SUB
    src_index = jnp.arange(devices, dtype=jnp.int32)
    src_row = src_index // N_SUB
    peer_row = jnp.arange(N_LEAF, dtype=jnp.int32)
    distance = jnp.abs(peer_row[None, :] - src_row[:, None])
    near_counts = jax.random.randint(jax.random.fold_in(key, 41), (devices, N_LEAF), CAP // 2, CAP + 1)
    far_counts = jax.random.randint(jax.random.fold_in(key, 42), (devices, N_LEAF), 1, CAP_FAR + 1)
    counts = jnp.where(distance == 0, 0, jnp.where(distance == 1, near_counts, far_counts))
    far_target = (src_row + 2 + jax.random.randint(jax.random.fold_in(key, 43), (devices,), 0, N_LEAF - 3)) % N_LEAF
    counts = jnp.where(peer_row[None, :] == far_target[:, None], CAP_FAR, counts)
    side_step = jax.random.randint(jax.random.fold_in(key, 44), (devices,), 0, 2) * 2 - 1
    side_step = jnp.where(src_row == 0, 1, jnp.where(src_row == N_LEAF - 1, -1, side_step))
    counts = jnp.where(peer_row[None, :] == (src_row + side_step)[:, None], CAP, counts)
    scores = jax.random.randint(jax.random.fold_in(key, 45), (devices, N_LEAF, LEAF_DEV), 0, 4096) * LEAF_DEV
    scores = scores + jnp.arange(LEAF_DEV, dtype=jnp.int32)
    ranking = jnp.argsort(scores, axis=-1)[:, :, :CAP].astype(jnp.int32)
    send_slots = jnp.where(jnp.arange(CAP, dtype=jnp.int32)[None, None, :] < counts[:, :, None], ranking, -1)
    incoming = send_slots.reshape(N_LEAF, N_SUB, N_LEAF, CAP).transpose(2, 1, 0, 3).reshape(devices, N_LEAF * CAP)
    recv_live = incoming >= 0
    row_span = N_SUB * LEAF_DEV
    recv_columns = jnp.where(recv_live, row_span + jnp.arange(N_LEAF * CAP, dtype=jnp.int32)[None, :], -1)

    def entries(salt, width):
        total_slots = LEAF_DEV * width
        entry_kind = jax.random.randint(jax.random.fold_in(key, salt), (devices, total_slots), 0, 10)
        row_pick = jax.random.randint(jax.random.fold_in(key, salt + 1), (devices, total_slots), 0, row_span)
        slot_pick = jax.random.randint(jax.random.fold_in(key, salt + 2), (devices, total_slots), 0, N_LEAF * CAP)
        recv_pick = jnp.take_along_axis(recv_columns, slot_pick, axis=1)
        base_values = jnp.where(entry_kind < 6, row_pick, jnp.where(entry_kind < 8, recv_pick, -1))
        place_scores = jax.random.randint(jax.random.fold_in(key, salt + 3), (devices, total_slots), 0, 4096) * total_slots
        place_scores = place_scores + jnp.arange(total_slots, dtype=jnp.int32)
        places = jnp.argsort(place_scores, axis=1)[:, :N_LEAF * CAP].astype(jnp.int32)
        places = jnp.where(recv_live, places, total_slots)

        def fill_device(row_values, targets, inserted):
            return row_values.at[targets].set(inserted, mode='drop')
        filled = jax.vmap(fill_device)(base_values, places, recv_columns)
        return filled.reshape(devices * LEAF_DEV, width).astype(jnp.int32)
    leaf_ids = jnp.arange(devices * LEAF_DEV, dtype=jnp.int32)
    own_column = leaf_ids // LEAF_DEV % N_SUB * LEAF_DEV + leaf_ids % LEAF_DEV
    near_list = jnp.concatenate([own_column[:, None], entries(50, NEAR - 1)], axis=1)
    far_list = entries(60, FAR)
    return (send_slots, near_list, far_list)


def draw_positions(key, part):
    key = jax.random.fold_in(key, 1)
    corners = cell_corners(jax.random.fold_in(key, 2))
    spread = jax.random.uniform(jax.random.fold_in(key, 3), (3, NB, LEAVES), jnp.float32)
    offsets = 0.01 + 0.98 * spread
    return corners[:, None, :] + offsets


def draw_near_list(key, part):
    send_slots, near_list, far_list = plan_tables(key)
    return near_list


def draw_far_list(key, part):
    send_slots, near_list, far_list = plan_tables(key)
    return far_list


def draw_send_slots(key, part):
    send_slots, near_list, far_list = plan_tables(key)
    return send_slots


def shard_levels(rng, dims, split, least, high):
    level = 1.0
    for position, shards_of in split:
        heights = jax.random.uniform(jax.random.fold_in(jax.random.fold_in(rng, 6), position), (shards_of,), jnp.float32, least / len(split), high / len(split))
        level = level * jnp.repeat(jnp.exp(heights), dims[position] // shards_of).reshape((-1,) + (1,) * (len(dims) - 1 - position))
    return level


def gaussian(own_key, shape, scale, bound, cuts=(), held_as=jnp.bfloat16):
    level = shard_levels(own_key, shape, cuts, -0.22, 0.18) if cuts else 1.0
    values = jax.random.normal(own_key, shape, jnp.float32) * scale * level
    return jnp.minimum(jnp.maximum(values, -bound), bound).astype(held_as)


def setup_inputs(seed: int = 0) -> dict:
    key_of = jax.random.split(jax.random.key(seed), 7)
    return {
        "positions": draw_positions(jax.random.fold_in(key_of[6], 71), 0),
        "charges": gaussian(key_of[1], (NB, LEAVES), 0.2, 1.6, ((1, 512),), jnp.float32),
        "m2l_ops": gaussian(key_of[2], (NODES, NODES * FAR), 4 ** -0.5, 3.0, (), jnp.float32),
        "near_list": draw_near_list(jax.random.fold_in(key_of[6], 71), 0),
        "far_list": draw_far_list(jax.random.fold_in(key_of[6], 71), 0),
        "send_slots": draw_send_slots(jax.random.fold_in(key_of[6], 71), 0),
    }


SOFTENING = 0.0625
HIGHEST = lax.Precision.HIGHEST

def cheb_table():
    degrees = jnp.arange(ORDER, dtype=jnp.float32)
    angles = (2.0 * degrees[:, None] + 1.0) * degrees[None, :] * (math.pi / (2.0 * ORDER))
    weights = jnp.where(degrees[None, :] == 0.0, 1.0 / ORDER, 2.0 / ORDER)
    return jnp.cos(angles) * weights

def interp_factors(positions):
    scaled = 2.0 * (positions - jnp.floor(positions)) - 1.0
    table_values = cheb_table()
    factors = []
    for axis_id in range(3):
        coordinate = scaled[axis_id]
        polynomials = [jnp.ones_like(coordinate), coordinate]
        for degree in range(2, ORDER):
            polynomials.append(2.0 * coordinate * polynomials[-1] - polynomials[-2])
        stacked = jnp.stack(polynomials[:ORDER])
        factors.append(jnp.einsum('nk,kjl->njl', table_values, stacked, precision=HIGHEST))
    return factors

def to_moments(factors, charges):
    first_axis, second_axis, third_axis = factors
    pair_factor = second_axis[:, None] * third_axis[None, :]
    moments = jnp.einsum('ajl,bcjl->abcl', first_axis * charges[None], pair_factor, precision=HIGHEST)
    return moments.reshape(NODES, -1)

def to_bodies(factors, expansions):
    first_axis, second_axis, third_axis = factors
    node_grid = expansions.reshape(ORDER, ORDER, ORDER, -1)
    inner_sum = jnp.einsum('cjl,abcl->abjl', third_axis, node_grid, precision=HIGHEST)
    second = jnp.einsum('bjl,abjl->ajl', second_axis, inner_sum, precision=HIGHEST)
    return lax.optimization_barrier(jnp.sum(first_axis * second, axis=0))

def slot_term(target_pos, target_ids, source_pos, source_charge, source_ids):
    between = source_pos[:, :, None, :] - target_pos[:, None, :, :]
    distance_sq = lax.optimization_barrier(jnp.sum(between * between, axis=0)) + SOFTENING
    kernel = 1.0 / jnp.sqrt(distance_sq)
    same_body = jnp.eye(NB, dtype=jnp.bool_)[:, :, None] & (source_ids == target_ids)[None, None, :]
    kernel = jnp.where(same_body, 0.0, kernel)
    return lax.optimization_barrier(jnp.sum(source_charge[:, None, :] * kernel, axis=0))

def resolve(entries, send_slots):
    leaves = entries.shape[0]
    leaf_ids = jnp.arange(leaves, dtype=jnp.int32)
    device = leaf_ids // LEAF_DEV
    row_idx = device // N_SUB
    sub_idx = device % N_SUB
    row_span = N_SUB * LEAF_DEV
    remote = jnp.maximum(entries - row_span, 0)
    peer_row = remote // CAP
    slot_idx = remote % CAP
    sender = peer_row * N_SUB + sub_idx[:, None]
    sent_slot = send_slots[sender, jnp.broadcast_to(row_idx[:, None], entries.shape), slot_idx]
    in_row = row_idx[:, None] * row_span + entries
    remote_ids = sender * LEAF_DEV + sent_slot
    return jnp.where(entries < 0, -1, jnp.where(entries < row_span, in_row, remote_ids)).astype(jnp.int32)

def reference(positions, charges, m2l_ops, near_list, far_list, send_slots):
    leaves = positions.shape[2]
    near_ids = resolve(near_list, send_slots)
    far_ids = resolve(far_list, send_slots)
    block_size = math.gcd(leaves, 4096)
    block_count = leaves // block_size
    pos_blocks = positions.reshape(3, NB, block_count, block_size).transpose(2, 0, 1, 3)
    charge_blocks = charges.reshape(NB, block_count, block_size).transpose(1, 0, 2)

    def block_moments(pieces):
        return to_moments(interp_factors(pieces[0]), pieces[1])
    moments = lax.map(block_moments, (pos_blocks, charge_blocks))
    moments = moments.transpose(1, 0, 2).reshape(NODES, leaves)
    starts = jnp.arange(block_count, dtype=jnp.int32) * block_size
    near_blocks = near_ids.reshape(block_count, block_size, NEAR)
    far_blocks = far_ids.reshape(block_count, block_size, FAR)

    def block_potential(pieces):
        block_start, target_pos, near_rows, far_rows = pieces
        target_ids = block_start + jnp.arange(block_size, dtype=jnp.int32)

        def near_step(running, column):
            is_valid = column >= 0
            safe_index = jnp.maximum(column, 0)
            source_pos = positions[:, :, safe_index]
            source_q = jnp.where(is_valid[None, :], charges[:, safe_index], 0.0)
            return (running + slot_term(target_pos, target_ids, source_pos, source_q, column), None)
        near_total, _ = lax.scan(near_step, jnp.zeros((NB, block_size), jnp.float32), near_rows.T)
        far_valid = far_rows >= 0
        gathered = moments[:, jnp.maximum(far_rows, 0)]
        gathered = jnp.where(far_valid.T[None], gathered.transpose(0, 2, 1), 0.0)
        flat = gathered.reshape(NODES * FAR, block_size)
        expansions = jnp.dot(m2l_ops, flat, precision=HIGHEST, preferred_element_type=jnp.float32)
        return near_total + to_bodies(interp_factors(target_pos), expansions)
    result = lax.map(block_potential, (starts, pos_blocks, near_blocks, far_blocks))
    return result.transpose(1, 0, 2).reshape(NB, leaves)
```

```python
import functools
import math

import jax
import jax.numpy as jnp
from jax import lax
from jax.experimental import pallas as pl
from jax.experimental.pallas import tpu as pltpu
from jax.sharding import PartitionSpec as P

NB = 32
ORDER = 6
NODES = 216
NEAR = 27
FAR = 16
CAP = 8
CAP_FAR = 3
SOFTENING = 0.0625
OWN = 256
PEERS = 128
ROW = 1024
RECV = PEERS * CAP_FAR
BESIDE = ROW + RECV
ZERO = BESIDE + 2 * CAP
TABLE = 1536
F32 = jnp.float32
BF16 = jnp.bfloat16


def factors_of(coordinate):
    x = 2.0 * (coordinate - jnp.floor(coordinate)) - 1.0
    polynomials = [None, x]
    for degree in range(2, ORDER):
        before = 1.0 if degree == 2 else polynomials[-2]
        polynomials.append(2.0 * x * polynomials[-1] - before)
    weight = lambda n, k: 2.0 / ORDER * math.cos(k * (2 * n + 1) * math.pi / 12)
    low, high = [], []
    for n in range(ORDER // 2):
        even = 1.0 / ORDER + weight(n, 4) * polynomials[4]
        if n != 1:
            even = even + weight(n, 2) * polynomials[2]
        odd = weight(n, 1) * x + weight(n, 3) * polynomials[3] + weight(n, 5) * polynomials[5]
        low.append(even + odd)
        high.append(even - odd)
    return low + high[::-1]


def fold_rows(parts):
    rows = lax.broadcasted_iota(jnp.int32, parts[0].shape, 0)
    for step in (4, 2, 1):
        first = (rows & step) == 0
        half = len(parts) // 2
        folded = []
        for n in range(half):
            p, q = parts[n], parts[n + half]
            kept = jnp.where(first, p, q)
            moved = jnp.where(first, q, p)
            if step == 4:
                folded.append(kept + pltpu.roll(moved, 4, 0))
            else:
                back = pltpu.roll(moved, step, 0)
                ahead = pltpu.roll(moved, 8 - step, 0)
                folded.append(kept + jnp.where(first, ahead, back))
        parts = folded
    return parts[0]


def moments_tile(table, start, cells, store):
    cells[...] = table[pl.ds(start, 128), :].T
    fx = factors_of(cells[0:32, :])
    fy = factors_of(cells[32:64, :])
    fz = factors_of(cells[64:96, :])
    charge = cells[96:128, :]
    parts = []
    node = 0
    for a in range(ORDER):
        qa = charge * fx[a]
        for b in range(ORDER):
            ab = qa * fy[b]
            for c in range(ORDER):
                abc = ab * fz[c]
                parts.append((abc[0:8] + abc[8:16]) + (abc[16:24] + abc[24:32]))
                node += 1
                if len(parts) == 8:
                    store(node - 8, fold_rows(parts))
                    parts = []


def local_kernel(
    near_idx, far_idx, rows, recv, beside, pos, charge, near_list, m2l,
    out, table, cells, moments, low_table, high_table,
    raw, near_cells, far_rows, far_flat, accum,
):
    table[0:ROW, :] = rows[...]
    table[ROW:BESIDE, :] = recv[...]
    table[BESIDE:ZERO, :] = beside[...]
    table[ZERO:TABLE, :] = jnp.zeros((TABLE - ZERO, 128), F32)
    moments[NODES:256, :] = jnp.zeros((256 - NODES, 128), F32)

    @pl.loop(0, TABLE // 128)
    def _(tile):
        start = pl.multiple_of(tile * 128, 128)

        def store(node, value):
            moments[node : node + 8, :] = value

        moments_tile(table, start, cells, store)
        low_table[pl.ds(start, 128), :] = moments[0:128, :].T
        high_table[pl.ds(start, 128), :] = moments[128:256, :].T

    out[...] = jnp.zeros((NB, OWN), F32)

    @pl.loop(0, NEAR)
    def _(k):
        for h in range(2):
            base = k * OWN + h * 128
            for i in range(128):
                raw[h, i : i + 1, :] = table[pl.ds(near_idx[base + i], 1), :]
            near_cells[h] = raw[h].T
            lanes = slice(h * 128, h * 128 + 128)
            tx, ty, tz = (pos[d * 32 : d * 32 + 32, lanes] for d in range(3))
            total = out[:, lanes]
            for a in range(NB):
                wide = lambda row: jnp.broadcast_to(near_cells[h, row : row + 1, :], (NB, 128))
                dx = wide(a) - tx
                dy = wide(32 + a) - ty
                dz = wide(64 + a) - tz
                square = (dx * dx + dy * dy) + (dz * dz + SOFTENING)
                total = total + wide(96 + a) * lax.rsqrt(square)
            out[:, lanes] = total

    @pl.loop(0, FAR)
    def _(k):
        for h in range(2):
            base = k * OWN + h * 128
            for i in range(128):
                cell = far_idx[base + i]
                far_rows[h, 0, i : i + 1, :] = low_table[pl.ds(cell, 1), :]
                far_rows[h, 1, i : i + 1, :] = high_table[pl.ds(cell, 1), :]
            flat = far_flat.at[h]
            flat[pl.ds(k, 128, stride=FAR), :] = far_rows[h, 0].T
            flat[pl.ds(k + 128 * FAR, NODES - 128, stride=FAR), :] = far_rows[h, 1].T[0 : NODES - 128]

    accum[...] = jnp.zeros((NODES, OWN), F32)
    for part in range(9):
        weights = m2l[:, part * 384 : part * 384 + 384]
        span = slice(part * 384, part * 384 + 384)
        values = jnp.concatenate([far_flat[0, span], far_flat[1, span]], axis=1)
        w_high = weights.astype(BF16)
        w_low = (weights - w_high.astype(F32)).astype(BF16)
        v_high = values.astype(BF16)
        v_low = (values - v_high.astype(F32)).astype(BF16)
        dot = functools.partial(jnp.dot, preferred_element_type=F32)
        accum[...] += dot(w_high, v_high) + (dot(w_high, v_low) + dot(w_low, v_high))

    own_first = lax.axis_index("sub") * OWN
    for h in range(2):
        lanes = slice(h * 128, h * 128 + 128)
        fx, fy, fz = (factors_of(pos[d * 32 : d * 32 + 32, lanes]) for d in range(3))
        wide = lambda row: jnp.broadcast_to(accum[row : row + 1, lanes], (NB, 128))
        total = out[:, lanes]
        for a in range(ORDER):
            for b in range(ORDER):
                inner = wide(a * 36 + b * 6) * fz[0]
                for c in range(1, ORDER):
                    inner = inner + wide(a * 36 + b * 6 + c) * fz[c]
                second = inner * fy[b] if b == 0 else second + inner * fy[b]
            total = total + second * fx[a]
        own = own_first + h * 128 + lax.broadcasted_iota(jnp.int32, (1, 128), 1)
        itself = (near_list[:, lanes] == own).astype(F32)
        count = jnp.sum(itself, axis=0, keepdims=True)
        out[:, lanes] = total - (4.0 * count) * charge[:, lanes]


def local_call(near_idx, far_idx, rows, recv, beside, pos, charge, near_list, m2l):
    vmem = pl.BlockSpec(memory_space=pltpu.VMEM)
    smem = pl.BlockSpec(memory_space=pltpu.SMEM)
    return pl.pallas_call(
        local_kernel,
        out_shape=jax.ShapeDtypeStruct((NB, OWN), F32),
        in_specs=[smem, smem] + [vmem] * 7,
        out_specs=vmem,
        scratch_shapes=[
            pltpu.VMEM((TABLE, 128), F32),
            pltpu.VMEM((128, 128), F32),
            pltpu.VMEM((256, 128), F32),
            pltpu.VMEM((TABLE, 128), F32),
            pltpu.VMEM((TABLE, 128), F32),
            pltpu.VMEM((2, 128, 128), F32),
            pltpu.VMEM((2, 128, 128), F32),
            pltpu.VMEM((2, 2, 128, 128), F32),
            pltpu.VMEM((2, NODES * FAR, 128), F32),
            pltpu.VMEM((NODES, OWN), F32),
        ],
        compiler_params=pltpu.CompilerParams(vmem_limit_bytes=40 * 2**20),
    )(near_idx, far_idx, rows, recv, beside, pos, charge, near_list, m2l)


def table_rows(entries, row_index):
    away = entries - ROW
    peer, slot = away >> 3, away & 7
    far = ROW + peer * CAP_FAR + jnp.minimum(slot, CAP_FAR - 1)
    left = BESIDE + slot
    remote = jnp.where(
        peer == row_index - 1, left, jnp.where(peer == row_index + 1, left + CAP, far)
    )
    return jnp.where(entries < 0, ZERO, jnp.where(entries < ROW, entries, remote))


def per_device(positions, charges, m2l_ops, near_list, far_list, send_slots):
    row_index = lax.axis_index("leaf")
    pos = positions.reshape(3 * NB, OWN)
    bodies = jnp.concatenate([pos, charges], axis=0).T
    rows = lax.all_gather(bodies, "sub", axis=0, tiled=True)
    slots = jnp.maximum(send_slots[0], 0)
    outgoing = jnp.take(bodies, slots[:, :CAP_FAR].reshape(-1), axis=0)
    recv = lax.all_to_all(
        outgoing.reshape(PEERS, CAP_FAR * 128), "leaf", split_axis=0, concat_axis=0, tiled=True
    ).reshape(RECV, 128)
    to_right = jnp.take(bodies, slots[jnp.minimum(row_index + 1, PEERS - 1)], axis=0)
    to_left = jnp.take(bodies, slots[jnp.maximum(row_index - 1, 0)], axis=0)
    ring = [(p, (p + 1) % PEERS) for p in range(PEERS)]
    from_left = lax.ppermute(to_right, "leaf", ring)
    from_right = lax.ppermute(to_left, "leaf", [(q, p) for p, q in ring])
    beside = jnp.concatenate([from_left, from_right], axis=0)
    near_t, far_t = near_list.T, far_list.T
    near_idx = table_rows(near_t, row_index).reshape(-1)
    far_idx = table_rows(far_t, row_index).reshape(-1)
    return local_call(near_idx, far_idx, rows, recv, beside, pos, charges, near_t, m2l_ops)


def solution(mesh):
    in_specs = (
        P(None, None, ("leaf", "sub")),
        P(None, ("leaf", "sub")),
        P(),
        P(("leaf", "sub"), None),
        P(("leaf", "sub"), None),
        P(("leaf", "sub"), None, None),
    )
    out_specs = P(None, ("leaf", "sub"))
    return jax.shard_map(
        per_device, mesh=mesh, in_specs=in_specs, out_specs=out_specs, check_vma=False
    )
```

```python
import functools
import math

import jax
import jax.numpy as jnp
from jax import lax
from jax.experimental import pallas as pl
from jax.experimental.pallas import tpu as pltpu
from jax.sharding import PartitionSpec as P

NB = 32
ORDER = 6
NODES = 216
NEAR = 27
FAR = 16
CAP = 8
CAP_FAR = 3
SOFTENING = 0.0625
OWN = 256
PEERS = 128
ROW = 1024
RECV = PEERS * CAP_FAR
BESIDE = ROW + RECV
ZERO = BESIDE + 2 * CAP
TABLE = 1536
F32 = jnp.float32
BF16 = jnp.bfloat16
MESH = pl.DeviceIdType.MESH


def factors_of(coordinate):
    x = 2.0 * (coordinate - jnp.floor(coordinate)) - 1.0
    polynomials = [None, x]
    for degree in range(2, ORDER):
        before = 1.0 if degree == 2 else polynomials[-2]
        polynomials.append(2.0 * x * polynomials[-1] - before)
    weight = lambda n, k: 2.0 / ORDER * math.cos(k * (2 * n + 1) * math.pi / 12)
    low, high = [], []
    for n in range(ORDER // 2):
        even = 1.0 / ORDER + weight(n, 4) * polynomials[4]
        if n != 1:
            even = even + weight(n, 2) * polynomials[2]
        odd = weight(n, 1) * x + weight(n, 3) * polynomials[3] + weight(n, 5) * polynomials[5]
        low.append(even + odd)
        high.append(even - odd)
    return low + high[::-1]


def fold_rows(parts):
    rows = lax.broadcasted_iota(jnp.int32, parts[0].shape, 0)
    for step in (4, 2, 1):
        first = (rows & step) == 0
        half = len(parts) // 2
        folded = []
        for n in range(half):
            p, q = parts[n], parts[n + half]
            kept = jnp.where(first, p, q)
            moved = jnp.where(first, q, p)
            if step == 4:
                folded.append(kept + pltpu.roll(moved, 4, 0))
            else:
                back = pltpu.roll(moved, step, 0)
                ahead = pltpu.roll(moved, 8 - step, 0)
                folded.append(kept + jnp.where(first, ahead, back))
        parts = folded
    return parts[0]


def table_rows(entries, row_index):
    away = entries - ROW
    peer, slot = away >> 3, away & 7
    far = ROW + peer * CAP_FAR + jnp.minimum(slot, CAP_FAR - 1)
    left = BESIDE + slot
    remote = jnp.where(
        peer == row_index - 1, left, jnp.where(peer == row_index + 1, left + CAP, far)
    )
    return jnp.where(entries < 0, ZERO, jnp.where(entries < ROW, entries, remote))


def split(value):
    high = value.astype(BF16)
    return high, (value - high.astype(F32)).astype(BF16)


def spread_tile(cell, spread, start):
    once, twice, thrice = (pltpu.roll(cell, n * 32, 1) for n in (1, 2, 3))
    which = lax.broadcasted_iota(jnp.int32, (64, 128), 1) >> 5
    odd, upper = (which & 1) == 1, (which & 2) == 2
    p, q = jnp.where(odd, once, cell), jnp.where(odd, thrice, twice)
    u, v = jnp.where(odd, cell, thrice), jnp.where(odd, twice, once)
    x = jnp.where(upper, q, p) - 1.0
    y = jnp.where(upper, v, u) - 1.0
    z = jnp.where(upper, p, q) - 1.0
    values = (-2.0 * x, -2.0 * y, -2.0 * z, x * x + y * y + z * z, jnp.where(upper, u, v))
    for f, value in enumerate(values):
        spread[pl.ds(start * 8 + f, 64, stride=8), :] = value


def moments_tile(table, spread, cells, moments, start):
    cells[...] = table[pl.ds(start, 128), :].T
    fx = factors_of(cells[0:32, :])
    fy = factors_of(cells[32:64, :])
    fz = factors_of(cells[64:96, :])
    charge = cells[96:128, :]
    parts = []
    node = 0
    for a in range(ORDER):
        qa = charge * fx[a]
        for b in range(ORDER):
            ab = qa * fy[b]
            for c in range(ORDER):
                abc = ab * fz[c]
                parts.append((abc[0:8] + abc[8:16]) + (abc[16:24] + abc[24:32]))
                node += 1
                if len(parts) == 8:
                    moments[node - 8 : node, :] = fold_rows(parts)
                    parts = []
    spread[pl.ds(start * 8 + 5, 128, stride=8), :] = moments[0:128, :].T
    spread[pl.ds(start * 8 + 6, 128, stride=8), :] = moments[128:256, :].T


def potential_kernel(
    pos, charge, near_list, far_list, slots, m2l_hbm,
    out,
    own, outgoing, beside_out, table, recv, beside, m2l,
    near_rows, far_rows, near_idx, far_idx,
    cells, moments, spread, near_sums, far_cells, op_table, operators, accum, expanded,
    local_sems, row_send, row_recv, leaf_send, leaf_recv, beside_send, beside_recv,
):
    row = lax.axis_index("leaf")
    sub = lax.axis_index("sub")
    own_first = sub * OWN
    barrier = pltpu.get_barrier_semaphore()

    @pl.loop(1, PEERS)
    def _(step):
        peer = lax.rem(row + step, PEERS)
        pl.semaphore_signal(barrier, inc=1, device_id=(peer, sub), device_id_type=MESH)

    for step in (1, 2, 3):
        pl.semaphore_signal(
            barrier, inc=1, device_id=(row, lax.rem(sub + step, 4)), device_id_type=MESH
        )

    fetch = pltpu.make_async_copy(m2l_hbm, m2l, local_sems.at[0])
    fetch.start()

    for h in range(2):
        lanes = slice(h * 128, h * 128 + 128)
        own[lanes, :] = jnp.concatenate([pos[:, lanes], charge[:, lanes]], axis=0).T

    @pl.loop(0, PEERS // 8)
    def _(block):
        for u in range(8):
            peer = block * 8 + u
            for c in range(CAP_FAR):
                slot = jnp.maximum(slots[c, peer], 0)
                outgoing[peer * CAP_FAR + c] = own[pl.ds(slot, 1), :]

    left, right = lax.rem(row + PEERS - 1, PEERS), lax.rem(row + 1, PEERS)
    for side, peer in enumerate((left, right)):
        for c in range(CAP):
            slot = jnp.maximum(slots[c, peer], 0)
            beside_out[side, c : c + 1, :] = own[pl.ds(slot, 1), :]

    pl.semaphore_wait(barrier, PEERS - 1 + 3)

    def row_copy(step):
        return pltpu.make_async_remote_copy(
            src_ref=own,
            dst_ref=table.at[pl.ds(pl.multiple_of(own_first, OWN), OWN)],
            send_sem=row_send.at[step - 1],
            recv_sem=row_recv.at[step - 1],
            device_id=(row, lax.rem(sub + step, 4)),
            device_id_type=MESH,
        )

    def leaf_copy(peer):
        return pltpu.make_async_remote_copy(
            src_ref=outgoing.at[pl.ds(peer * CAP_FAR, CAP_FAR)],
            dst_ref=recv.at[pl.ds(row * CAP_FAR, CAP_FAR)],
            send_sem=leaf_send,
            recv_sem=leaf_recv,
            device_id=(peer, sub),
            device_id_type=MESH,
        )

    def beside_copy(side, peer):
        return pltpu.make_async_remote_copy(
            src_ref=beside_out.at[side],
            dst_ref=beside.at[1 - side],
            send_sem=beside_send.at[side],
            recv_sem=beside_recv.at[1 - side],
            device_id=(peer, sub),
            device_id_type=MESH,
        )

    for step in (1, 3, 2):
        row_copy(step).start()

    @pl.loop(1, PEERS // 2)
    def _(step):
        leaf_copy(lax.rem(row + step, PEERS)).start()
        leaf_copy(lax.rem(row + PEERS - step, PEERS)).start()

    leaf_copy(lax.rem(row + PEERS // 2, PEERS)).start()
    beside_copy(0, left).start()
    beside_copy(1, right).start()

    near_rows[...] = table_rows(near_list[...], row)
    far_rows[...] = table_rows(far_list[...], row)
    near_move = pltpu.make_async_copy(near_rows, near_idx, local_sems.at[1])
    far_move = pltpu.make_async_copy(far_rows, far_idx, local_sems.at[2])
    near_move.start()
    far_move.start()

    fetch.wait()
    moments[NODES:256, :] = jnp.zeros((256 - NODES, 128), F32)
    op_table[:, NODES * FAR :, :] = jnp.zeros((2, (256 - NODES) * FAR, 128), F32)

    @pl.loop(0, NODES * FAR // 128)
    def _(tile):
        start = pl.multiple_of(tile * 128, 128)
        op_table[0, pl.ds(start, 128), :] = m2l[0:128, pl.ds(start, 128)].T
        rest = m2l[128:NODES, pl.ds(start, 128)].T
        op_table[1, pl.ds(start, 128), 0 : NODES - 128] = rest
        op_table[1, pl.ds(start, 128), NODES - 128 :] = jnp.zeros((128, 256 - NODES), F32)

    @pl.loop(0, FAR)
    def _(k):
        for half in range(2):
            plane = op_table.at[half]
            high, low = split(plane[pl.ds(k, 256, stride=FAR), :])
            operators[k, 0:256, half * 128 : half * 128 + 128] = high
            operators[k, 256:512, half * 128 : half * 128 + 128] = low

    def build(start):
        for part in range(2):
            at = pl.multiple_of(start + part * 64, 64)
            spread_tile(table[pl.ds(at, 64), :], spread, at)
        moments_tile(table, spread, cells, moments, start)

    table[pl.ds(pl.multiple_of(own_first, OWN), OWN), :] = own[...]
    for step in range(4):
        if step:
            row_copy(step).wait_recv()
        first = lax.rem(sub + 4 - step, 4) * OWN

        @pl.loop(0, 2)
        def _(tile):
            build(pl.multiple_of(first + tile * 128, 128))

    recv[pl.ds(row * CAP_FAR, CAP_FAR)] = jnp.zeros((CAP_FAR, 1, 128), F32)
    beside_copy(1, left).wait_recv()
    beside_copy(0, right).wait_recv()
    everything = pl.ds(0, (PEERS - 1) * CAP_FAR)
    pltpu.make_async_copy(recv.at[everything], recv.at[everything], leaf_recv).wait()
    blocks = table.reshape(TABLE // 8, 8, 128)

    @pl.loop(0, RECV // 8)
    def _(block):
        for u in range(8):
            blocks[ROW // 8 + block, u : u + 1, :] = recv[block * 8 + u]

    for side in range(2):
        table[BESIDE + side * CAP : BESIDE + side * CAP + CAP, :] = beside[side]
    table[ZERO:TABLE, :] = jnp.zeros((TABLE - ZERO, 128), F32)

    @pl.loop(ROW // 128, TABLE // 128)
    def _(tile):
        build(pl.multiple_of(tile * 128, 128))

    near_move.wait()
    far_move.wait()
    lane = lax.broadcasted_iota(jnp.int32, (8, 128), 1)
    group = lane >> 5
    target = group * 8 + lax.broadcasted_iota(jnp.int32, (8, 128), 0)
    spread_cells = spread.reshape(TABLE, 8, 128)

    @pl.loop(0, OWN // 8)
    def _(block):
        for u in range(8):
            i = block * 8 + u
            mine = jnp.broadcast_to(own[pl.ds(i, 1), :], (8, 128))
            tx, ty, tz = (
                jnp.take_along_axis(mine, target + 32 * d, axis=1, mode="promise_in_bounds") - 1.0
                for d in range(3)
            )
            level = (tx * tx + ty * ty) + (tz * tz + SOFTENING)
            sums = [None, None]
            for k in range(NEAR):
                cell = near_idx[k, i]
                wide = lambda f: jnp.broadcast_to(spread_cells[cell, f : f + 1, :], (8, 128))
                square = (wide(0) * tx + wide(1) * ty) + (wide(2) * tz + (wide(3) + level))
                term = wide(4) * lax.rsqrt(square)
                sums[k % 2] = term if k < 2 else sums[k % 2] + term
            near_sums[pl.ds(i, 8, stride=OWN), :] = sums[0] + sums[1]
            for k in range(FAR):
                far_cells[k, block, 2 * u : 2 * u + 2, :] = spread_cells[far_idx[k, i], 5:7, :]

    far_flat = far_cells.reshape(FAR * OWN * 2, 128)
    dot = functools.partial(jnp.dot, preferred_element_type=F32)
    accum[...] = jnp.zeros((OWN, 256), F32)

    @pl.loop(0, FAR // 2)
    def _(pair):
        total = accum[...]
        for n in range(2):
            k = pair * 2 + n
            values = jnp.concatenate(
                [far_flat[pl.ds(k * OWN * 2 + half, OWN, stride=2), :] for half in range(2)], axis=1
            )
            high, low = split(values)
            total = total + dot(jnp.concatenate([high, high], axis=1), operators[k])
            total = total + dot(low, operators[k, 0:256])
        accum[...] = total

    for h in range(2):
        for t in range(2):
            expanded[t * 128 : t * 128 + 128, h * 128 : h * 128 + 128] = accum[
                h * 128 : h * 128 + 128, t * 128 : t * 128 + 128
            ].T

    ones = (lax.broadcasted_iota(jnp.int32, (8, 128), 0) == group).astype(BF16)
    across = (((1,), (1,)), ((), ()))
    for s in range(8):
        high, low = split(near_sums[s * OWN : s * OWN + OWN, :])
        both = lax.dot_general(ones, high, across, preferred_element_type=F32) + lax.dot_general(
            ones, low, across, preferred_element_type=F32
        )
        for g in range(4):
            out[g * 8 + s : g * 8 + s + 1, :] = both[g : g + 1, :]

    for h in range(2):
        lanes = slice(h * 128, h * 128 + 128)
        fx, fy, fz = (factors_of(pos[d * 32 : d * 32 + 32, lanes]) for d in range(3))
        wide = lambda row: jnp.broadcast_to(expanded[row : row + 1, lanes], (NB, 128))
        total = out[:, lanes]
        for a in range(ORDER):
            for b in range(ORDER):
                inner = wide(a * 36 + b * 6) * fz[0]
                for c in range(1, ORDER):
                    inner = inner + wide(a * 36 + b * 6 + c) * fz[c]
                second = inner * fy[b] if b == 0 else second + inner * fy[b]
            total = total + second * fx[a]
        mine = own_first + h * 128 + lax.broadcasted_iota(jnp.int32, (1, 128), 1)
        itself = (near_list[:, lanes] == mine).astype(F32)
        count = jnp.sum(itself, axis=0, keepdims=True)
        out[:, lanes] = total - (4.0 * count) * charge[:, lanes]

    for step in (1, 2, 3):
        row_copy(step).wait_send()
    beside_copy(0, left).wait_send()
    beside_copy(1, right).wait_send()
    pltpu.make_async_copy(outgoing.at[everything], outgoing.at[everything], leaf_send).wait()


def potential_call(pos, charge, near_list, far_list, slots, m2l):
    vmem = pl.BlockSpec(memory_space=pltpu.VMEM)
    smem = pl.BlockSpec(memory_space=pltpu.SMEM)
    dma = pltpu.SemaphoreType.DMA
    return pl.pallas_call(
        potential_kernel,
        out_shape=jax.ShapeDtypeStruct((NB, OWN), F32),
        in_specs=[vmem, vmem, vmem, vmem, smem, pl.BlockSpec(memory_space=pl.ANY)],
        out_specs=vmem,
        scratch_shapes=[
            pltpu.VMEM((OWN, 128), F32),
            pltpu.VMEM((RECV, 1, 128), F32),
            pltpu.VMEM((2, CAP, 128), F32),
            pltpu.VMEM((TABLE, 128), F32),
            pltpu.VMEM((RECV, 1, 128), F32),
            pltpu.VMEM((2, CAP, 128), F32),
            pltpu.VMEM((NODES, NODES * FAR), F32),
            pltpu.VMEM((NEAR, OWN), jnp.int32),
            pltpu.VMEM((FAR, OWN), jnp.int32),
            pltpu.SMEM((NEAR, OWN), jnp.int32),
            pltpu.SMEM((FAR, OWN), jnp.int32),
            pltpu.VMEM((128, 128), F32),
            pltpu.VMEM((256, 128), F32),
            pltpu.VMEM((TABLE * 8, 128), F32),
            pltpu.VMEM((8 * OWN, 128), F32),
            pltpu.VMEM((FAR, OWN // 8, 16, 128), F32),
            pltpu.VMEM((2, 256 * FAR, 128), F32),
            pltpu.VMEM((FAR, 512, 256), BF16),
            pltpu.VMEM((OWN, 256), F32),
            pltpu.VMEM((256, OWN), F32),
            dma((3,)),
            dma((3,)),
            dma((3,)),
            dma,
            dma,
            dma((2,)),
            dma((2,)),
        ],
        compiler_params=pltpu.CompilerParams(
            collective_id=0, has_side_effects=True, vmem_limit_bytes=48 * 2**20
        ),
    )(pos, charge, near_list, far_list, slots, m2l)


def per_device(positions, charges, m2l_ops, near_list, far_list, send_slots):
    pos = positions.reshape(3 * NB, OWN)
    return potential_call(pos, charges, near_list.T, far_list.T, send_slots[0].T, m2l_ops)


def solution(mesh):
    in_specs = (
        P(None, None, ("leaf", "sub")),
        P(None, ("leaf", "sub")),
        P(),
        P(("leaf", "sub"), None),
        P(("leaf", "sub"), None),
        P(("leaf", "sub"), None, None),
    )
    out_specs = P(None, ("leaf", "sub"))
    return jax.shard_map(
        per_device, mesh=mesh, in_specs=in_specs, out_specs=out_specs, check_vma=False
    )
```

```python
import functools
import math

import jax
import jax.numpy as jnp
from jax import lax
from jax.experimental import pallas as pl
from jax.experimental.pallas import tpu as pltpu
from jax.sharding import PartitionSpec as P

NB = 32
ORDER = 6
NODES = 216
NEAR = 27
FAR = 16
CAP = 8
CAP_FAR = 3
SOFTENING = 0.0625
OWN = 256
PEERS = 128
PLANE = 8
LINE = 16
ROW = 1024
RECV = PEERS * CAP_FAR
BESIDE = ROW + RECV
ZERO = BESIDE + 2 * CAP
TABLE = 1536
F32 = jnp.float32
BF16 = jnp.bfloat16
MESH = pl.DeviceIdType.MESH


def factors_of(coordinate):
    x = 2.0 * (coordinate - jnp.floor(coordinate)) - 1.0
    polynomials = [None, x]
    for degree in range(2, ORDER):
        before = 1.0 if degree == 2 else polynomials[-2]
        polynomials.append(2.0 * x * polynomials[-1] - before)
    weight = lambda n, k: 2.0 / ORDER * math.cos(k * (2 * n + 1) * math.pi / 12)
    low, high = [], []
    for n in range(ORDER // 2):
        even = 1.0 / ORDER + weight(n, 4) * polynomials[4]
        if n != 1:
            even = even + weight(n, 2) * polynomials[2]
        odd = weight(n, 1) * x + weight(n, 3) * polynomials[3] + weight(n, 5) * polynomials[5]
        low.append(even + odd)
        high.append(even - odd)
    return low + high[::-1]


def fold_rows(parts):
    rows = lax.broadcasted_iota(jnp.int32, parts[0].shape, 0)
    for step in (4, 2, 1):
        first = (rows & step) == 0
        half = len(parts) // 2
        folded = []
        for n in range(half):
            p, q = parts[n], parts[n + half]
            kept = jnp.where(first, p, q)
            moved = jnp.where(first, q, p)
            if step == 4:
                folded.append(kept + pltpu.roll(moved, 4, 0))
            else:
                back = pltpu.roll(moved, step, 0)
                ahead = pltpu.roll(moved, 8 - step, 0)
                folded.append(kept + jnp.where(first, ahead, back))
        parts = folded
    return parts[0]


def table_rows(entries, row_index):
    away = entries - ROW
    peer, slot = away >> 3, away & 7
    far = ROW + peer * CAP_FAR + jnp.minimum(slot, CAP_FAR - 1)
    left = BESIDE + slot
    remote = jnp.where(
        peer == row_index - 1, left, jnp.where(peer == row_index + 1, left + CAP, far)
    )
    return jnp.where(entries < 0, ZERO, jnp.where(entries < ROW, entries, remote))


def split(value):
    high = value.astype(BF16)
    return high, (value - high.astype(F32)).astype(BF16)


def spread_tile(cell, spread, start):
    once, twice, thrice = (pltpu.roll(cell, n * 32, 1) for n in (1, 2, 3))
    which = lax.broadcasted_iota(jnp.int32, (64, 128), 1) >> 5
    odd, upper = (which & 1) == 1, (which & 2) == 2
    p, q = jnp.where(odd, once, cell), jnp.where(odd, thrice, twice)
    u, v = jnp.where(odd, cell, thrice), jnp.where(odd, twice, once)
    x = jnp.where(upper, q, p) - 1.0
    y = jnp.where(upper, v, u) - 1.0
    z = jnp.where(upper, p, q) - 1.0
    values = (-2.0 * x, -2.0 * y, -2.0 * z, x * x + y * y + z * z, jnp.where(upper, u, v))
    for f, value in enumerate(values):
        spread[pl.ds(start * 8 + f, 64, stride=8), :] = value


def moments_tile(table, spread, cells, moments, start):
    cells[...] = table[pl.ds(start, 128), :].T
    fx = factors_of(cells[0:32, :])
    fy = factors_of(cells[32:64, :])
    fz = factors_of(cells[64:96, :])
    charge = cells[96:128, :]
    parts = []
    node = 0
    for a in range(ORDER):
        qa = charge * fx[a]
        for b in range(ORDER):
            ab = qa * fy[b]
            for c in range(ORDER):
                abc = ab * fz[c]
                parts.append((abc[0:8] + abc[8:16]) + (abc[16:24] + abc[24:32]))
                node += 1
                if len(parts) == 8:
                    moments[node - 8 : node, :] = fold_rows(parts)
                    parts = []
    spread[pl.ds(start * 8 + 5, 128, stride=8), :] = moments[0:128, :].T
    spread[pl.ds(start * 8 + 6, 128, stride=8), :] = moments[128:256, :].T


def potential_kernel(
    pos_hbm, charge_hbm, near_hbm, far_hbm, slots_hbm, m2l_hbm,
    out,
    bodies, near_list, far_list, slots, own, outgoing, stage, beside_out, table, recv, beside, m2l,
    near_rows, far_rows, near_idx, far_idx,
    cells, moments, spread, near_sums, far_cells, op_table, operators, accum, expanded,
    local_sems, list_sems, row_send, row_recv, plane_send, plane_recv, line_send, line_recv,
    beside_send, beside_recv,
):
    row = lax.axis_index("leaf")
    sub = lax.axis_index("sub")
    line, plane = row // PLANE, row % PLANE
    own_first = sub * OWN
    left, right = lax.rem(row + PEERS - 1, PEERS), lax.rem(row + 1, PEERS)

    def in_plane(step):
        return line * PLANE + lax.rem(plane + step, PLANE)

    def on_line(step):
        return lax.rem(line + step, LINE) * PLANE + plane

    barrier = pltpu.get_barrier_semaphore()

    def greet(peer, peer_sub):
        pl.semaphore_signal(barrier, inc=1, device_id=(peer, peer_sub), device_id_type=MESH)

    for step in range(1, PLANE):
        greet(in_plane(step), sub)
    for step in range(1, LINE):
        greet(on_line(step), sub)
    for step in (1, 2, 3):
        greet(row, lax.rem(sub + step, 4))
    greet(left, sub)
    greet(right, sub)

    fetches = [
        pltpu.make_async_copy(source, target, local_sems.at[n])
        for n, (source, target) in enumerate(
            [
                (pos_hbm, bodies.at[0:96]),
                (charge_hbm, bodies.at[96:128]),
                (slots_hbm, slots),
                (near_hbm, near_list),
                (far_hbm, far_list),
                (m2l_hbm, m2l),
            ]
        )
    ]
    for fetch in fetches:
        fetch.start()
    fetches[0].wait()
    fetches[1].wait()

    for h in range(2):
        lanes = slice(h * 128, h * 128 + 128)
        own[lanes, :] = bodies[:, lanes].T

    fetches[2].wait()

    @pl.loop(0, LINE)
    def _(far_line):
        for peer_plane in range(PLANE):
            for c in range(CAP_FAR):
                slot = jnp.maximum(slots[c, far_line * PLANE + peer_plane], 0)
                outgoing[peer_plane, far_line, c] = own[pl.ds(slot, 1), :]

    for side, peer in enumerate((left, right)):
        for c in range(CAP):
            slot = jnp.maximum(slots[c, peer], 0)
            beside_out[side, c : c + 1, :] = own[pl.ds(slot, 1), :]

    pl.semaphore_wait(barrier, PLANE - 1 + LINE - 1 + 3 + 2)

    def row_copy(step):
        return pltpu.make_async_remote_copy(
            src_ref=own,
            dst_ref=table.at[pl.ds(pl.multiple_of(own_first, OWN), OWN)],
            send_sem=row_send.at[step - 1],
            recv_sem=row_recv.at[step - 1],
            device_id=(row, lax.rem(sub + step, 4)),
            device_id_type=MESH,
        )

    def plane_copy(step):
        peer = in_plane(step)
        return pltpu.make_async_remote_copy(
            src_ref=outgoing.at[peer % PLANE],
            dst_ref=stage.at[plane],
            send_sem=plane_send,
            recv_sem=plane_recv,
            device_id=(peer, sub),
            device_id_type=MESH,
        )

    def line_copy(step):
        peer = on_line(step)
        return pltpu.make_async_remote_copy(
            src_ref=stage.at[:, peer // PLANE],
            dst_ref=recv.at[line],
            send_sem=line_send,
            recv_sem=line_recv,
            device_id=(peer, sub),
            device_id_type=MESH,
        )

    def wait_all(blocks, count, sem):
        some = blocks.at[pl.ds(0, count)]
        pltpu.make_async_copy(some, some, sem).wait()

    def beside_copy(side, peer):
        return pltpu.make_async_remote_copy(
            src_ref=beside_out.at[side],
            dst_ref=beside.at[1 - side],
            send_sem=beside_send.at[side],
            recv_sem=beside_recv.at[1 - side],
            device_id=(peer, sub),
            device_id_type=MESH,
        )

    for step in range(1, PLANE):
        plane_copy(step).start()
    for step in (1, 3, 2):
        row_copy(step).start()
    beside_copy(0, left).start()
    beside_copy(1, right).start()

    @pl.loop(0, LINE)
    def _(far_line):
        for c in range(CAP_FAR):
            stage[plane, far_line, c] = outgoing[plane, far_line, c]

    fetches[3].wait()
    fetches[4].wait()
    for entries, rows in ((near_list, near_rows), (far_list, far_rows)):
        named = table_rows(entries[...], row)
        for k in range(rows.shape[0]):
            rows[k] = named[k : k + 1, :]
    moves = [
        pltpu.make_async_copy(
            rows.at[k, 0], flat.at[pl.ds(k * OWN, OWN)], list_sems.at[first + k]
        )
        for rows, flat, first, count in ((near_rows, near_idx, 0, NEAR), (far_rows, far_idx, NEAR, FAR))
        for k in range(count)
    ]
    for move in moves:
        move.start()

    def build(start):
        for part in range(2):
            at = pl.multiple_of(start + part * 64, 64)
            spread_tile(table[pl.ds(at, 64), :], spread, at)
        moments_tile(table, spread, cells, moments, start)

    def build_row(first):
        @pl.loop(0, 2)
        def _(tile):
            build(pl.multiple_of(first + tile * 128, 128))

    moments[NODES:256, :] = jnp.zeros((256 - NODES, 128), F32)
    table[pl.ds(pl.multiple_of(own_first, OWN), OWN), :] = own[...]
    build_row(own_first)

    wait_all(stage, PLANE - 1, plane_recv)
    for step in range(1, LINE // 2):
        line_copy(step).start()
        line_copy(LINE - step).start()
    line_copy(LINE // 2).start()
    for peer_plane in range(PLANE):
        for c in range(CAP_FAR):
            recv[line, peer_plane, c] = stage[peer_plane, line, c]

    fetches[5].wait()
    op_table[:, NODES * FAR :, :] = jnp.zeros((2, (256 - NODES) * FAR, 128), F32)

    @pl.loop(0, NODES * FAR // 128)
    def _(tile):
        start = pl.multiple_of(tile * 128, 128)
        op_table[0, pl.ds(start, 128), :] = m2l[0:128, pl.ds(start, 128)].T
        rest = m2l[128:NODES, pl.ds(start, 128)].T
        op_table[1, pl.ds(start, 128), 0 : NODES - 128] = rest
        op_table[1, pl.ds(start, 128), NODES - 128 :] = jnp.zeros((128, 256 - NODES), F32)

    @pl.loop(0, FAR)
    def _(k):
        for half in range(2):
            plane = op_table.at[half]
            high, low = split(plane[pl.ds(k, 256, stride=FAR), :])
            operators[k, 0:256, half * 128 : half * 128 + 128] = high
            operators[k, 256:512, half * 128 : half * 128 + 128] = low

    for step in (1, 3, 2):
        row_copy(step).wait_recv()
        build_row(lax.rem(sub + 4 - step, 4) * OWN)

    beside_copy(1, left).wait_recv()
    beside_copy(0, right).wait_recv()
    wait_all(recv, LINE - 1, line_recv)
    blocks = table.reshape(TABLE // 8, 8, 128)

    @pl.loop(0, LINE)
    def _(far_line):
        for n in range(PLANE * CAP_FAR):
            blocks[ROW // 8 + far_line * PLANE * CAP_FAR // 8 + n // 8, n % 8 : n % 8 + 1, :] = recv[
                far_line, n // CAP_FAR, n % CAP_FAR
            ]

    for side in range(2):
        table[BESIDE + side * CAP : BESIDE + side * CAP + CAP, :] = beside[side]
    table[ZERO:TABLE, :] = jnp.zeros((TABLE - ZERO, 128), F32)

    @pl.loop(ROW // 128, TABLE // 128)
    def _(tile):
        build(pl.multiple_of(tile * 128, 128))

    for move in moves:
        move.wait()
    lane = lax.broadcasted_iota(jnp.int32, (8, 128), 1)
    group = lane >> 5
    target = group * 8 + lax.broadcasted_iota(jnp.int32, (8, 128), 0)
    spread_cells = spread.reshape(TABLE, 8, 128)

    def near_leaf(i):
        mine = jnp.broadcast_to(own[pl.ds(i, 1), :], (8, 128))
        tx, ty, tz = (
            jnp.take_along_axis(mine, target + 32 * d, axis=1, mode="promise_in_bounds") - 1.0
            for d in range(3)
        )
        level = (tx * tx + ty * ty) + (tz * tz + SOFTENING)
        sums = [None, None]
        for k in range(NEAR):
            cell = near_idx[k * OWN + i]
            wide = lambda f: jnp.broadcast_to(spread_cells[cell, f : f + 1, :], (8, 128))
            square = (wide(0) * tx + wide(1) * ty) + (wide(2) * tz + (wide(3) + level))
            term = wide(4) * lax.rsqrt(square)
            sums[k % 2] = term if k < 2 else sums[k % 2] + term
        near_sums[pl.ds(i, 8, stride=OWN), :] = sums[0] + sums[1]

    @pl.loop(0, OWN // 16)
    def _(block):
        for u in range(8):
            near_leaf(block * 8 + u)
            for half in range(2):
                for k in range(FAR):
                    cell = far_idx[k * OWN + half * (OWN // 2) + block * 8 + u]
                    far_cells[k, half * (OWN // 16) + block, 2 * u : 2 * u + 2, :] = spread_cells[
                        cell, 5:7, :
                    ]

    far_flat = far_cells.reshape(FAR * OWN * 2, 128)
    dot = functools.partial(jnp.dot, preferred_element_type=F32)
    accum[...] = jnp.zeros((OWN, 256), F32)

    @pl.loop(0, FAR)
    def _(k):
        values = jnp.concatenate(
            [far_flat[pl.ds(k * OWN * 2 + half, OWN, stride=2), :] for half in range(2)], axis=1
        )
        high, low = split(values)
        accum[...] += dot(jnp.concatenate([high, high], axis=1), operators[k]) + dot(
            low, operators[k, 0:256]
        )
        for u in range(8):
            near_leaf(OWN // 2 + k * 8 + u)

    for h in range(2):
        for t in range(2):
            expanded[t * 128 : t * 128 + 128, h * 128 : h * 128 + 128] = accum[
                h * 128 : h * 128 + 128, t * 128 : t * 128 + 128
            ].T

    ones = (lax.broadcasted_iota(jnp.int32, (8, 128), 0) == group).astype(BF16)
    across = (((1,), (1,)), ((), ()))
    for s in range(8):
        high, low = split(near_sums[s * OWN : s * OWN + OWN, :])
        both = lax.dot_general(ones, high, across, preferred_element_type=F32) + lax.dot_general(
            ones, low, across, preferred_element_type=F32
        )
        for g in range(4):
            out[g * 8 + s : g * 8 + s + 1, :] = both[g : g + 1, :]

    for h in range(2):
        lanes = slice(h * 128, h * 128 + 128)
        fx, fy, fz = (factors_of(bodies[d * 32 : d * 32 + 32, lanes]) for d in range(3))
        wide = lambda row: jnp.broadcast_to(expanded[row : row + 1, lanes], (NB, 128))
        total = out[:, lanes]
        for a in range(ORDER):
            for b in range(ORDER):
                inner = wide(a * 36 + b * 6) * fz[0]
                for c in range(1, ORDER):
                    inner = inner + wide(a * 36 + b * 6 + c) * fz[c]
                second = inner * fy[b] if b == 0 else second + inner * fy[b]
            total = total + second * fx[a]
        mine = own_first + h * 128 + lax.broadcasted_iota(jnp.int32, (1, 128), 1)
        itself = (near_list[:, lanes] == mine).astype(F32)
        count = jnp.sum(itself, axis=0, keepdims=True)
        out[:, lanes] = total - (4.0 * count) * bodies[96:128, lanes]

    for step in (1, 2, 3):
        row_copy(step).wait_send()
    beside_copy(0, left).wait_send()
    beside_copy(1, right).wait_send()
    wait_all(outgoing, PLANE - 1, plane_send)
    wait_all(recv, LINE - 1, line_send)


def potential_call(pos, charge, near_list, far_list, slots, m2l):
    vmem = pl.BlockSpec(memory_space=pltpu.VMEM)
    dma = pltpu.SemaphoreType.DMA
    return pl.pallas_call(
        potential_kernel,
        out_shape=jax.ShapeDtypeStruct((NB, OWN), F32),
        in_specs=[pl.BlockSpec(memory_space=pl.ANY)] * 6,
        out_specs=vmem,
        scratch_shapes=[
            pltpu.VMEM((128, OWN), F32),
            pltpu.VMEM((NEAR, OWN), jnp.int32),
            pltpu.VMEM((FAR, OWN), jnp.int32),
            pltpu.SMEM((CAP, PEERS), jnp.int32),
            pltpu.VMEM((OWN, 128), F32),
            pltpu.VMEM((PLANE, LINE, CAP_FAR, 1, 128), F32),
            pltpu.VMEM((PLANE, LINE, CAP_FAR, 1, 128), F32),
            pltpu.VMEM((2, CAP, 128), F32),
            pltpu.VMEM((TABLE, 128), F32),
            pltpu.VMEM((LINE, PLANE, CAP_FAR, 1, 128), F32),
            pltpu.VMEM((2, CAP, 128), F32),
            pltpu.VMEM((NODES, NODES * FAR), F32),
            pltpu.VMEM((NEAR, 1, OWN), jnp.int32),
            pltpu.VMEM((FAR, 1, OWN), jnp.int32),
            pltpu.SMEM((NEAR * OWN,), jnp.int32),
            pltpu.SMEM((FAR * OWN,), jnp.int32),
            pltpu.VMEM((128, 128), F32),
            pltpu.VMEM((256, 128), F32),
            pltpu.VMEM((TABLE * 8, 128), F32),
            pltpu.VMEM((8 * OWN, 128), F32),
            pltpu.VMEM((FAR, OWN // 8, 16, 128), F32),
            pltpu.VMEM((2, 256 * FAR, 128), F32),
            pltpu.VMEM((FAR, 512, 256), BF16),
            pltpu.VMEM((OWN, 256), F32),
            pltpu.VMEM((256, OWN), F32),
            dma((6,)),
            dma((NEAR + FAR,)),
            dma((3,)),
            dma((3,)),
            dma,
            dma,
            dma,
            dma,
            dma((2,)),
            dma((2,)),
        ],
        compiler_params=pltpu.CompilerParams(
            collective_id=0, has_side_effects=True, vmem_limit_bytes=60 * 2**20
        ),
    )(pos, charge, near_list, far_list, slots, m2l)


def per_device(positions, charges, m2l_ops, near_list, far_list, send_slots):
    pos = positions.reshape(3 * NB, OWN)
    return potential_call(pos, charges, near_list.T, far_list.T, send_slots[0].T, m2l_ops)


def solution(mesh):
    in_specs = (
        P(None, None, ("leaf", "sub")),
        P(None, ("leaf", "sub")),
        P(),
        P(("leaf", "sub"), None),
        P(("leaf", "sub"), None),
        P(("leaf", "sub"), None, None),
    )
    out_specs = P(None, ("leaf", "sub"))
    return jax.shard_map(
        per_device, mesh=mesh, in_specs=in_specs, out_specs=out_specs, check_vma=False
    )
```

```python
import functools
import math

import jax
import jax.numpy as jnp
from jax import lax
from jax.experimental import pallas as pl
from jax.experimental.pallas import tpu as pltpu
from jax.sharding import PartitionSpec as P

NB = 32
ORDER = 6
NODES = 216
NEAR = 27
FAR = 16
CAP = 8
CAP_FAR = 3
SOFTENING = 0.0625
OWN = 256
PEERS = 128
PLANE = 8
LINE = 16
ROW = 1024
RECV = PEERS * CAP_FAR
BESIDE = ROW + RECV
ZERO = BESIDE + 2 * CAP
TABLE = 1536
F32 = jnp.float32
BF16 = jnp.bfloat16
MESH = pl.DeviceIdType.MESH


def factors_of(coordinate):
    x = 2.0 * (coordinate - jnp.floor(coordinate)) - 1.0
    polynomials = [None, x]
    for degree in range(2, ORDER):
        before = 1.0 if degree == 2 else polynomials[-2]
        polynomials.append(2.0 * x * polynomials[-1] - before)
    weight = lambda n, k: 2.0 / ORDER * math.cos(k * (2 * n + 1) * math.pi / 12)
    low, high = [], []
    for n in range(ORDER // 2):
        even = 1.0 / ORDER + weight(n, 4) * polynomials[4]
        if n != 1:
            even = even + weight(n, 2) * polynomials[2]
        odd = weight(n, 1) * x + weight(n, 3) * polynomials[3] + weight(n, 5) * polynomials[5]
        low.append(even + odd)
        high.append(even - odd)
    return low + high[::-1]


def fold_rows(parts):
    rows = lax.broadcasted_iota(jnp.int32, parts[0].shape, 0)
    for step in (4, 2, 1):
        first = (rows & step) == 0
        half = len(parts) // 2
        folded = []
        for n in range(half):
            p, q = parts[n], parts[n + half]
            kept = jnp.where(first, p, q)
            moved = jnp.where(first, q, p)
            if step == 4:
                folded.append(kept + pltpu.roll(moved, 4, 0))
            else:
                back = pltpu.roll(moved, step, 0)
                ahead = pltpu.roll(moved, 8 - step, 0)
                folded.append(kept + jnp.where(first, ahead, back))
        parts = folded
    return parts[0]


def table_rows(entries, row_index):
    away = entries - ROW
    peer, slot = away >> 3, away & 7
    far = ROW + peer * CAP_FAR + jnp.minimum(slot, CAP_FAR - 1)
    left = BESIDE + slot
    remote = jnp.where(
        peer == row_index - 1, left, jnp.where(peer == row_index + 1, left + CAP, far)
    )
    return jnp.where(entries < 0, ZERO, jnp.where(entries < ROW, entries, remote))


def split(value):
    high = value.astype(BF16)
    return high, (value - high.astype(F32)).astype(BF16)


def spread_tile(cell, spread, start):
    once, twice, thrice = (pltpu.roll(cell, n * 32, 1) for n in (1, 2, 3))
    which = lax.broadcasted_iota(jnp.int32, (64, 128), 1) >> 5
    odd, upper = (which & 1) == 1, (which & 2) == 2
    p, q = jnp.where(odd, once, cell), jnp.where(odd, thrice, twice)
    u, v = jnp.where(odd, cell, thrice), jnp.where(odd, twice, once)
    x = jnp.where(upper, q, p) - 1.0
    y = jnp.where(upper, v, u) - 1.0
    z = jnp.where(upper, p, q) - 1.0
    values = (-2.0 * x, -2.0 * y, -2.0 * z, x * x + y * y + z * z, jnp.where(upper, u, v))
    for f, value in enumerate(values):
        spread[pl.ds(start * 8 + f, 64, stride=8), :] = value


def moments_tile(table, spread, cells, moments, start):
    cells[...] = table[pl.ds(start, 128), :].T
    fx = factors_of(cells[0:32, :])
    fy = factors_of(cells[32:64, :])
    fz = factors_of(cells[64:96, :])
    charge = cells[96:128, :]
    parts = []
    node = 0
    for a in range(ORDER):
        qa = charge * fx[a]
        for b in range(ORDER):
            ab = qa * fy[b]
            for c in range(ORDER):
                abc = ab * fz[c]
                parts.append((abc[0:8] + abc[8:16]) + (abc[16:24] + abc[24:32]))
                node += 1
                if len(parts) == 8:
                    moments[node - 8 : node, :] = fold_rows(parts)
                    parts = []
    spread[pl.ds(start * 8 + 5, 128, stride=8), :] = moments[0:128, :].T
    spread[pl.ds(start * 8 + 6, 128, stride=8), :] = moments[128:256, :].T


def potential_kernel(
    pos_hbm, charge_hbm, near_hbm, far_hbm, slots_hbm, m2l_hbm,
    out,
    bodies, near_list, far_list, slots, own, outgoing, stage, beside_out, table, recv, beside, m2l,
    near_rows, far_rows, near_idx, far_idx,
    cells, moments, spread, near_sums, far_cells, op_table, operators, accum, expanded,
    local_sems, list_sems, row_send, row_recv, plane_send, plane_recv, line_send, line_recv,
    beside_send, beside_recv,
):
    row = lax.axis_index("leaf")
    sub = lax.axis_index("sub")
    line, plane = row // PLANE, row % PLANE
    own_first = sub * OWN
    left, right = lax.rem(row + PEERS - 1, PEERS), lax.rem(row + 1, PEERS)

    def in_plane(step):
        return line * PLANE + lax.rem(plane + step, PLANE)

    def on_line(step):
        return lax.rem(line + step, LINE) * PLANE + plane

    barrier = pltpu.get_barrier_semaphore()

    def greet(peer, peer_sub):
        pl.semaphore_signal(barrier, inc=1, device_id=(peer, peer_sub), device_id_type=MESH)

    for step in range(1, PLANE):
        greet(in_plane(step), sub)
    for step in range(1, LINE):
        greet(on_line(step), sub)
    for step in (1, 2, 3):
        greet(row, lax.rem(sub + step, 4))
    greet(left, sub)
    greet(right, sub)

    fetches = [
        pltpu.make_async_copy(source, target, local_sems.at[n])
        for n, (source, target) in enumerate(
            [
                (pos_hbm, bodies.at[0:96]),
                (charge_hbm, bodies.at[96:128]),
                (slots_hbm, slots),
                (near_hbm, near_list),
                (far_hbm, far_list),
                (m2l_hbm, m2l),
            ]
        )
    ]
    for fetch in fetches:
        fetch.start()
    fetches[0].wait()
    fetches[1].wait()

    for h in range(2):
        lanes = slice(h * 128, h * 128 + 128)
        own[lanes, :] = bodies[:, lanes].T

    fetches[2].wait()

    @pl.loop(0, LINE)
    def _(far_line):
        for peer_plane in range(PLANE):
            for c in range(CAP_FAR):
                slot = jnp.maximum(slots[c, far_line * PLANE + peer_plane], 0)
                outgoing[peer_plane, far_line, c] = own[pl.ds(slot, 1), :]

    for side, peer in enumerate((left, right)):
        for c in range(CAP):
            slot = jnp.maximum(slots[c, peer], 0)
            beside_out[side, c : c + 1, :] = own[pl.ds(slot, 1), :]

    pl.semaphore_wait(barrier, PLANE - 1 + LINE - 1 + 3 + 2)

    def row_copy(step):
        return pltpu.make_async_remote_copy(
            src_ref=own,
            dst_ref=table.at[pl.ds(pl.multiple_of(own_first, OWN), OWN)],
            send_sem=row_send.at[step - 1],
            recv_sem=row_recv.at[step - 1],
            device_id=(row, lax.rem(sub + step, 4)),
            device_id_type=MESH,
        )

    def plane_copy(step):
        peer = in_plane(step)
        return pltpu.make_async_remote_copy(
            src_ref=outgoing.at[peer % PLANE],
            dst_ref=stage.at[plane],
            send_sem=plane_send,
            recv_sem=plane_recv,
            device_id=(peer, sub),
            device_id_type=MESH,
        )

    def line_copy(step):
        peer = on_line(step)
        return pltpu.make_async_remote_copy(
            src_ref=stage.at[:, peer // PLANE],
            dst_ref=recv.at[line],
            send_sem=line_send,
            recv_sem=line_recv,
            device_id=(peer, sub),
            device_id_type=MESH,
        )

    def wait_all(blocks, count, sem):
        some = blocks.at[pl.ds(0, count)]
        pltpu.make_async_copy(some, some, sem).wait()

    def beside_copy(side, peer):
        return pltpu.make_async_remote_copy(
            src_ref=beside_out.at[side],
            dst_ref=beside.at[1 - side],
            send_sem=beside_send.at[side],
            recv_sem=beside_recv.at[1 - side],
            device_id=(peer, sub),
            device_id_type=MESH,
        )

    for step in range(1, PLANE):
        plane_copy(step).start()
    for step in (1, 3, 2):
        row_copy(step).start()
    beside_copy(0, left).start()
    beside_copy(1, right).start()

    @pl.loop(0, LINE)
    def _(far_line):
        for c in range(CAP_FAR):
            stage[plane, far_line, c] = outgoing[plane, far_line, c]

    fetches[3].wait()
    fetches[4].wait()
    for entries, rows in ((near_list, near_rows), (far_list, far_rows)):
        named = table_rows(entries[...], row)
        for k in range(rows.shape[0]):
            rows[k] = named[k : k + 1, :]
    moves = [
        pltpu.make_async_copy(
            rows.at[k, 0], flat.at[pl.ds(k * OWN, OWN)], list_sems.at[first + k]
        )
        for rows, flat, first, count in ((near_rows, near_idx, 0, NEAR), (far_rows, far_idx, NEAR, FAR))
        for k in range(count)
    ]
    for move in moves:
        move.start()

    def build(start):
        for part in range(2):
            at = pl.multiple_of(start + part * 64, 64)
            spread_tile(table[pl.ds(at, 64), :], spread, at)
        moments_tile(table, spread, cells, moments, start)

    def build_row(first):
        @pl.loop(0, 2)
        def _(tile):
            build(pl.multiple_of(first + tile * 128, 128))

    moments[NODES:256, :] = jnp.zeros((256 - NODES, 128), F32)
    table[pl.ds(pl.multiple_of(own_first, OWN), OWN), :] = own[...]
    build_row(own_first)

    wait_all(stage, PLANE - 1, plane_recv)
    for step in range(1, LINE // 2):
        line_copy(step).start()
        line_copy(LINE - step).start()
    line_copy(LINE // 2).start()
    for peer_plane in range(PLANE):
        for c in range(CAP_FAR):
            recv[line, peer_plane, c] = stage[peer_plane, line, c]

    fetches[5].wait()
    op_table[:, NODES * FAR :, :] = jnp.zeros((2, (256 - NODES) * FAR, 128), F32)

    @pl.loop(0, NODES * FAR // 128, unroll=3)
    def _(tile):
        start = pl.multiple_of(tile * 128, 128)
        op_table[0, pl.ds(start, 128), :] = m2l[0:128, pl.ds(start, 128)].T
        rest = m2l[128:NODES, pl.ds(start, 128)].T
        op_table[1, pl.ds(start, 128), 0 : NODES - 128] = rest
        op_table[1, pl.ds(start, 128), NODES - 128 :] = jnp.zeros((128, 256 - NODES), F32)

    @pl.loop(0, FAR, unroll=2)
    def _(k):
        for half in range(2):
            plane = op_table.at[half]
            high, low = split(plane[pl.ds(k, 256, stride=FAR), :])
            operators[k, 0:256, half * 128 : half * 128 + 128] = high
            operators[k, 256:512, half * 128 : half * 128 + 128] = low

    for step in (1, 3, 2):
        row_copy(step).wait_recv()
        build_row(lax.rem(sub + 4 - step, 4) * OWN)

    beside_copy(1, left).wait_recv()
    beside_copy(0, right).wait_recv()
    wait_all(recv, LINE - 1, line_recv)
    blocks = table.reshape(TABLE // 8, 8, 128)

    @pl.loop(0, LINE)
    def _(far_line):
        for n in range(PLANE * CAP_FAR):
            blocks[ROW // 8 + far_line * PLANE * CAP_FAR // 8 + n // 8, n % 8 : n % 8 + 1, :] = recv[
                far_line, n // CAP_FAR, n % CAP_FAR
            ]

    for side in range(2):
        table[BESIDE + side * CAP : BESIDE + side * CAP + CAP, :] = beside[side]
    table[ZERO:TABLE, :] = jnp.zeros((TABLE - ZERO, 128), F32)

    @pl.loop(ROW // 128, TABLE // 128)
    def _(tile):
        build(pl.multiple_of(tile * 128, 128))

    for move in moves:
        move.wait()
    lane = lax.broadcasted_iota(jnp.int32, (8, 128), 1)
    group = lane >> 5
    target = group * 8 + lax.broadcasted_iota(jnp.int32, (8, 128), 0)
    spread_cells = spread.reshape(TABLE, 8, 128)

    def near_leaf(i):
        mine = jnp.broadcast_to(own[pl.ds(i, 1), :], (8, 128))
        tx, ty, tz = (
            jnp.take_along_axis(mine, target + 32 * d, axis=1, mode="promise_in_bounds") - 1.0
            for d in range(3)
        )
        level = (tx * tx + ty * ty) + (tz * tz + SOFTENING)
        sums = [None, None]
        for k in range(NEAR):
            cell = near_idx[k * OWN + i]
            wide = lambda f: jnp.broadcast_to(spread_cells[cell, f : f + 1, :], (8, 128))
            square = (wide(0) * tx + wide(1) * ty) + (wide(2) * tz + (wide(3) + level))
            term = wide(4) * lax.rsqrt(square)
            sums[k % 2] = term if k < 2 else sums[k % 2] + term
        near_sums[pl.ds(i, 8, stride=OWN), :] = sums[0] + sums[1]

    @pl.loop(0, OWN // 8, unroll=2)
    def _(block):
        for u in range(8):
            i = block * 8 + u
            near_leaf(i)
            for k in range(FAR):
                cell = far_idx[k * OWN + i]
                far_cells[k, block, 2 * u : 2 * u + 2, :] = spread_cells[cell, 5:7, :]

    far_flat = far_cells.reshape(FAR * OWN * 2, 128)
    dot = functools.partial(jnp.dot, preferred_element_type=F32)
    accum[...] = jnp.zeros((OWN, 256), F32)

    @pl.loop(0, FAR // 2)
    def _(pair):
        total = accum[...]
        for n in range(2):
            k = pair * 2 + n
            values = jnp.concatenate(
                [far_flat[pl.ds(k * OWN * 2 + half, OWN, stride=2), :] for half in range(2)], axis=1
            )
            high, low = split(values)
            total = total + dot(jnp.concatenate([high, high], axis=1), operators[k])
            total = total + dot(low, operators[k, 0:256])
        accum[...] = total

    for h in range(2):
        for t in range(2):
            expanded[t * 128 : t * 128 + 128, h * 128 : h * 128 + 128] = accum[
                h * 128 : h * 128 + 128, t * 128 : t * 128 + 128
            ].T

    ones = (lax.broadcasted_iota(jnp.int32, (8, 128), 0) == group).astype(BF16)
    across = (((1,), (1,)), ((), ()))
    for s in range(8):
        high, low = split(near_sums[s * OWN : s * OWN + OWN, :])
        both = lax.dot_general(ones, high, across, preferred_element_type=F32) + lax.dot_general(
            ones, low, across, preferred_element_type=F32
        )
        for g in range(4):
            out[g * 8 + s : g * 8 + s + 1, :] = both[g : g + 1, :]

    for h in range(2):
        lanes = slice(h * 128, h * 128 + 128)
        fx, fy, fz = (factors_of(bodies[d * 32 : d * 32 + 32, lanes]) for d in range(3))
        wide = lambda row: jnp.broadcast_to(expanded[row : row + 1, lanes], (NB, 128))
        total = out[:, lanes]
        for a in range(ORDER):
            for b in range(ORDER):
                inner = wide(a * 36 + b * 6) * fz[0]
                for c in range(1, ORDER):
                    inner = inner + wide(a * 36 + b * 6 + c) * fz[c]
                second = inner * fy[b] if b == 0 else second + inner * fy[b]
            total = total + second * fx[a]
        mine = own_first + h * 128 + lax.broadcasted_iota(jnp.int32, (1, 128), 1)
        itself = (near_list[:, lanes] == mine).astype(F32)
        count = jnp.sum(itself, axis=0, keepdims=True)
        out[:, lanes] = total - (4.0 * count) * bodies[96:128, lanes]

    for step in (1, 2, 3):
        row_copy(step).wait_send()
    beside_copy(0, left).wait_send()
    beside_copy(1, right).wait_send()
    wait_all(outgoing, PLANE - 1, plane_send)
    wait_all(recv, LINE - 1, line_send)


def potential_call(pos, charge, near_list, far_list, slots, m2l):
    vmem = pl.BlockSpec(memory_space=pltpu.VMEM)
    dma = pltpu.SemaphoreType.DMA
    return pl.pallas_call(
        potential_kernel,
        out_shape=jax.ShapeDtypeStruct((NB, OWN), F32),
        in_specs=[pl.BlockSpec(memory_space=pl.ANY)] * 6,
        out_specs=vmem,
        scratch_shapes=[
            pltpu.VMEM((128, OWN), F32),
            pltpu.VMEM((NEAR, OWN), jnp.int32),
            pltpu.VMEM((FAR, OWN), jnp.int32),
            pltpu.SMEM((CAP, PEERS), jnp.int32),
            pltpu.VMEM((OWN, 128), F32),
            pltpu.VMEM((PLANE, LINE, CAP_FAR, 1, 128), F32),
            pltpu.VMEM((PLANE, LINE, CAP_FAR, 1, 128), F32),
            pltpu.VMEM((2, CAP, 128), F32),
            pltpu.VMEM((TABLE, 128), F32),
            pltpu.VMEM((LINE, PLANE, CAP_FAR, 1, 128), F32),
            pltpu.VMEM((2, CAP, 128), F32),
            pltpu.VMEM((NODES, NODES * FAR), F32),
            pltpu.VMEM((NEAR, 1, OWN), jnp.int32),
            pltpu.VMEM((FAR, 1, OWN), jnp.int32),
            pltpu.SMEM((NEAR * OWN,), jnp.int32),
            pltpu.SMEM((FAR * OWN,), jnp.int32),
            pltpu.VMEM((128, 128), F32),
            pltpu.VMEM((256, 128), F32),
            pltpu.VMEM((TABLE * 8, 128), F32),
            pltpu.VMEM((8 * OWN, 128), F32),
            pltpu.VMEM((FAR, OWN // 8, 16, 128), F32),
            pltpu.VMEM((2, 256 * FAR, 128), F32),
            pltpu.VMEM((FAR, 512, 256), BF16),
            pltpu.VMEM((OWN, 256), F32),
            pltpu.VMEM((256, OWN), F32),
            dma((6,)),
            dma((NEAR + FAR,)),
            dma((3,)),
            dma((3,)),
            dma,
            dma,
            dma,
            dma,
            dma((2,)),
            dma((2,)),
        ],
        compiler_params=pltpu.CompilerParams(
            collective_id=0, has_side_effects=True, vmem_limit_bytes=60 * 2**20
        ),
    )(pos, charge, near_list, far_list, slots, m2l)


def per_device(positions, charges, m2l_ops, near_list, far_list, send_slots):
    pos = positions.reshape(3 * NB, OWN)
    return potential_call(pos, charges, near_list.T, far_list.T, send_slots[0].T, m2l_ops)


def solution(mesh):
    in_specs = (
        P(None, None, ("leaf", "sub")),
        P(None, ("leaf", "sub")),
        P(),
        P(("leaf", "sub"), None),
        P(("leaf", "sub"), None),
        P(("leaf", "sub"), None, None),
    )
    out_specs = P(None, ("leaf", "sub"))
    return jax.shard_map(
        per_device, mesh=mesh, in_specs=in_specs, out_specs=out_specs, check_vma=False
    )
```

```python
import functools
import math

import jax
import jax.numpy as jnp
from jax import lax
from jax.experimental import pallas as pl
from jax.experimental.pallas import tpu as pltpu
from jax.sharding import PartitionSpec as P

NB = 32
ORDER = 6
NODES = 216
NEAR = 27
FAR = 16
CAP = 8
CAP_FAR = 3
SOFTENING = 0.0625
OWN = 256
PEERS = 128
PLANE = 8
LINE = 16
ROW = 1024
RECV = PEERS * CAP_FAR
BESIDE = ROW + RECV
ZERO = BESIDE + 2 * CAP
TABLE = 1536
F32 = jnp.float32
BF16 = jnp.bfloat16
MESH = pl.DeviceIdType.MESH


def factors_of(coordinate):
    x = 2.0 * (coordinate - jnp.floor(coordinate)) - 1.0
    polynomials = [None, x]
    for degree in range(2, ORDER):
        before = 1.0 if degree == 2 else polynomials[-2]
        polynomials.append(2.0 * x * polynomials[-1] - before)
    weight = lambda n, k: 2.0 / ORDER * math.cos(k * (2 * n + 1) * math.pi / 12)
    low, high = [], []
    for n in range(ORDER // 2):
        even = 1.0 / ORDER + weight(n, 4) * polynomials[4]
        if n != 1:
            even = even + weight(n, 2) * polynomials[2]
        odd = weight(n, 1) * x + weight(n, 3) * polynomials[3] + weight(n, 5) * polynomials[5]
        low.append(even + odd)
        high.append(even - odd)
    return low + high[::-1]


def fold_rows(parts):
    rows = lax.broadcasted_iota(jnp.int32, parts[0].shape, 0)
    for step in (4, 2, 1):
        first = (rows & step) == 0
        half = len(parts) // 2
        folded = []
        for n in range(half):
            p, q = parts[n], parts[n + half]
            kept = jnp.where(first, p, q)
            moved = jnp.where(first, q, p)
            if step == 4:
                folded.append(kept + pltpu.roll(moved, 4, 0))
            else:
                back = pltpu.roll(moved, step, 0)
                ahead = pltpu.roll(moved, 8 - step, 0)
                folded.append(kept + jnp.where(first, ahead, back))
        parts = folded
    return parts[0]


def table_rows(entries, row_index):
    away = entries - ROW
    peer, slot = away >> 3, away & 7
    far = ROW + peer * CAP_FAR + jnp.minimum(slot, CAP_FAR - 1)
    left = BESIDE + slot
    remote = jnp.where(
        peer == row_index - 1, left, jnp.where(peer == row_index + 1, left + CAP, far)
    )
    return jnp.where(entries < 0, ZERO, jnp.where(entries < ROW, entries, remote))


def split(value):
    high = value.astype(BF16)
    return high, (value - high.astype(F32)).astype(BF16)


def spread_tile(cell, spread, start):
    once, twice, thrice = (pltpu.roll(cell, n * 32, 1) for n in (1, 2, 3))
    which = lax.broadcasted_iota(jnp.int32, (64, 128), 1) >> 5
    odd, upper = (which & 1) == 1, (which & 2) == 2
    p, q = jnp.where(odd, once, cell), jnp.where(odd, thrice, twice)
    u, v = jnp.where(odd, cell, thrice), jnp.where(odd, twice, once)
    x = jnp.where(upper, q, p) - 1.0
    y = jnp.where(upper, v, u) - 1.0
    z = jnp.where(upper, p, q) - 1.0
    values = (-2.0 * x, -2.0 * y, -2.0 * z, x * x + y * y + z * z, jnp.where(upper, u, v))
    for f, value in enumerate(values):
        spread[pl.ds(start * 8 + f, 64, stride=8), :] = value


def moments_tile(table, spread, cells, moments, start):
    cells[...] = table[pl.ds(start, 128), :].T
    fx = factors_of(cells[0:32, :])
    fy = factors_of(cells[32:64, :])
    fz = factors_of(cells[64:96, :])
    charge = cells[96:128, :]
    parts = []
    node = 0
    for a in range(ORDER):
        qa = charge * fx[a]
        for b in range(ORDER):
            ab = qa * fy[b]
            for c in range(ORDER):
                abc = ab * fz[c]
                parts.append((abc[0:8] + abc[8:16]) + (abc[16:24] + abc[24:32]))
                node += 1
                if len(parts) == 8:
                    moments[node - 8 : node, :] = fold_rows(parts)
                    parts = []
    spread[pl.ds(start * 8 + 5, 128, stride=8), :] = moments[0:128, :].T
    spread[pl.ds(start * 8 + 6, 128, stride=8), :] = moments[128:256, :].T


def potential_kernel(
    pos_hbm, charge_hbm, near_hbm, far_hbm, slots_hbm, m2l_hbm,
    out,
    bodies, near_list, far_list, slots, own, outgoing, stage, beside_out, table, recv, beside, m2l,
    near_rows, far_rows, near_idx, far_idx,
    cells, moments, spread, near_sums, far_cells, op_table, operators, accum, expanded,
    local_sems, list_sems, row_send, row_recv, plane_send, plane_recv, line_send, line_recv,
    beside_send, beside_recv,
):
    row = lax.axis_index("leaf")
    sub = lax.axis_index("sub")
    line, plane = row // PLANE, row % PLANE
    own_first = sub * OWN
    left, right = lax.rem(row + PEERS - 1, PEERS), lax.rem(row + 1, PEERS)

    def in_plane(step):
        return line * PLANE + lax.rem(plane + step, PLANE)

    def on_line(step):
        return lax.rem(line + step, LINE) * PLANE + plane

    barrier = pltpu.get_barrier_semaphore()

    def greet(peer, peer_sub):
        pl.semaphore_signal(barrier, inc=1, device_id=(peer, peer_sub), device_id_type=MESH)

    for step in range(1, PLANE):
        greet(in_plane(step), sub)
    for step in range(1, LINE):
        greet(on_line(step), sub)
    for step in (1, 2, 3):
        greet(row, lax.rem(sub + step, 4))
    greet(left, sub)
    greet(right, sub)

    fetches = [
        pltpu.make_async_copy(source, target, local_sems.at[n])
        for n, (source, target) in enumerate(
            [
                (pos_hbm, bodies.at[0:96]),
                (charge_hbm, bodies.at[96:128]),
                (slots_hbm, slots),
                (near_hbm, near_list),
                (far_hbm, far_list),
                (m2l_hbm, m2l),
            ]
        )
    ]
    for fetch in fetches:
        fetch.start()
    fetches[0].wait()
    fetches[1].wait()

    for h in range(2):
        lanes = slice(h * 128, h * 128 + 128)
        own[lanes, :] = bodies[:, lanes].T

    fetches[2].wait()

    @pl.loop(0, LINE)
    def _(far_line):
        for peer_plane in range(PLANE):
            for c in range(CAP_FAR):
                slot = jnp.maximum(slots[c, far_line * PLANE + peer_plane], 0)
                outgoing[peer_plane, far_line, c] = own[pl.ds(slot, 1), :]

    for side, peer in enumerate((left, right)):
        for c in range(CAP):
            slot = jnp.maximum(slots[c, peer], 0)
            beside_out[side, c : c + 1, :] = own[pl.ds(slot, 1), :]

    pl.semaphore_wait(barrier, PLANE - 1 + LINE - 1 + 3 + 2)

    def row_copy(step):
        return pltpu.make_async_remote_copy(
            src_ref=own,
            dst_ref=table.at[pl.ds(pl.multiple_of(own_first, OWN), OWN)],
            send_sem=row_send.at[step - 1],
            recv_sem=row_recv.at[step - 1],
            device_id=(row, lax.rem(sub + step, 4)),
            device_id_type=MESH,
        )

    def plane_copy(step):
        peer = in_plane(step)
        return pltpu.make_async_remote_copy(
            src_ref=outgoing.at[peer % PLANE],
            dst_ref=stage.at[plane],
            send_sem=plane_send,
            recv_sem=plane_recv,
            device_id=(peer, sub),
            device_id_type=MESH,
        )

    def line_copy(step):
        peer = on_line(step)
        return pltpu.make_async_remote_copy(
            src_ref=stage.at[:, peer // PLANE],
            dst_ref=recv.at[line],
            send_sem=line_send,
            recv_sem=line_recv,
            device_id=(peer, sub),
            device_id_type=MESH,
        )

    def wait_all(blocks, count, sem):
        some = blocks.at[pl.ds(0, count)]
        pltpu.make_async_copy(some, some, sem).wait()

    def beside_copy(side, peer):
        return pltpu.make_async_remote_copy(
            src_ref=beside_out.at[side],
            dst_ref=beside.at[1 - side],
            send_sem=beside_send.at[side],
            recv_sem=beside_recv.at[1 - side],
            device_id=(peer, sub),
            device_id_type=MESH,
        )

    for step in range(1, PLANE):
        plane_copy(step).start()
    for step in (1, 3, 2):
        row_copy(step).start()
    beside_copy(0, left).start()
    beside_copy(1, right).start()

    @pl.loop(0, LINE)
    def _(far_line):
        for c in range(CAP_FAR):
            stage[plane, far_line, c] = outgoing[plane, far_line, c]

    fetches[3].wait()
    fetches[4].wait()
    for entries, rows in ((near_list, near_rows), (far_list, far_rows)):
        named = table_rows(entries[...], row)
        for k in range(rows.shape[0]):
            rows[k] = named[k : k + 1, :]
    moves = [
        pltpu.make_async_copy(
            rows.at[k, 0], flat.at[pl.ds(k * OWN, OWN)], list_sems.at[first + k]
        )
        for rows, flat, first, count in ((near_rows, near_idx, 0, NEAR), (far_rows, far_idx, NEAR, FAR))
        for k in range(count)
    ]
    for move in moves:
        move.start()

    def build(start, m):
        for part in range(2):
            at = pl.multiple_of(start + part * 64, 64)
            spread_tile(table[pl.ds(at, 64), :], spread, at)
        moments_tile(table, spread, cells.at[m], moments.at[m], start)

    def build_row(first):
        for tile in range(2):
            build(pl.multiple_of(first + tile * 128, 128), tile)

    moments[:, NODES:256, :] = jnp.zeros((2, 256 - NODES, 128), F32)
    table[pl.ds(pl.multiple_of(own_first, OWN), OWN), :] = own[...]
    build_row(own_first)

    wait_all(stage, PLANE - 1, plane_recv)
    for step in range(1, LINE // 2):
        line_copy(step).start()
        line_copy(LINE - step).start()
    line_copy(LINE // 2).start()
    for peer_plane in range(PLANE):
        for c in range(CAP_FAR):
            recv[line, peer_plane, c] = stage[peer_plane, line, c]

    fetches[5].wait()
    op_table[:, NODES * FAR :, :] = jnp.zeros((2, (256 - NODES) * FAR, 128), F32)

    @pl.loop(0, NODES * FAR // 128, unroll=3)
    def _(tile):
        start = pl.multiple_of(tile * 128, 128)
        op_table[0, pl.ds(start, 128), :] = m2l[0:128, pl.ds(start, 128)].T
        rest = m2l[128:NODES, pl.ds(start, 128)].T
        op_table[1, pl.ds(start, 128), 0 : NODES - 128] = rest
        op_table[1, pl.ds(start, 128), NODES - 128 :] = jnp.zeros((128, 256 - NODES), F32)

    @pl.loop(0, FAR, unroll=2)
    def _(k):
        for half in range(2):
            plane = op_table.at[half]
            high, low = split(plane[pl.ds(k, 256, stride=FAR), :])
            operators[k, 0:256, half * 128 : half * 128 + 128] = high
            operators[k, 256:512, half * 128 : half * 128 + 128] = low

    for step in (1, 3, 2):
        row_copy(step).wait_recv()
        build_row(lax.rem(sub + 4 - step, 4) * OWN)

    beside_copy(1, left).wait_recv()
    beside_copy(0, right).wait_recv()
    wait_all(recv, LINE - 1, line_recv)
    blocks = table.reshape(TABLE // 8, 8, 128)

    @pl.loop(0, LINE)
    def _(far_line):
        for n in range(PLANE * CAP_FAR):
            blocks[ROW // 8 + far_line * PLANE * CAP_FAR // 8 + n // 8, n % 8 : n % 8 + 1, :] = recv[
                far_line, n // CAP_FAR, n % CAP_FAR
            ]

    for side in range(2):
        table[BESIDE + side * CAP : BESIDE + side * CAP + CAP, :] = beside[side]
    table[ZERO:TABLE, :] = jnp.zeros((TABLE - ZERO, 128), F32)

    @pl.loop(ROW // 256, TABLE // 256)
    def _(pair):
        for tile in range(2):
            build(pl.multiple_of(pair * 256 + tile * 128, 128), tile)

    for move in moves:
        move.wait()
    lane = lax.broadcasted_iota(jnp.int32, (8, 128), 1)
    group = lane >> 5
    target = group * 8 + lax.broadcasted_iota(jnp.int32, (8, 128), 0)
    spread_cells = spread.reshape(TABLE, 8, 128)

    def near_leaf(i):
        mine = jnp.broadcast_to(own[pl.ds(i, 1), :], (8, 128))
        tx, ty, tz = (
            jnp.take_along_axis(mine, target + 32 * d, axis=1, mode="promise_in_bounds") - 1.0
            for d in range(3)
        )
        level = (tx * tx + ty * ty) + (tz * tz + SOFTENING)
        sums = [None, None]
        for k in range(NEAR):
            cell = near_idx[k * OWN + i]
            wide = lambda f: jnp.broadcast_to(spread_cells[cell, f : f + 1, :], (8, 128))
            square = (wide(0) * tx + wide(1) * ty) + (wide(2) * tz + (wide(3) + level))
            term = wide(4) * lax.rsqrt(square)
            sums[k % 2] = term if k < 2 else sums[k % 2] + term
        near_sums[pl.ds(i, 8, stride=OWN), :] = sums[0] + sums[1]

    @pl.loop(0, OWN // 8, unroll=2)
    def _(block):
        for u in range(8):
            i = block * 8 + u
            near_leaf(i)
            for k in range(FAR):
                cell = far_idx[k * OWN + i]
                far_cells[k, block, 2 * u : 2 * u + 2, :] = spread_cells[cell, 5:7, :]

    far_flat = far_cells.reshape(FAR * OWN * 2, 128)
    dot = functools.partial(jnp.dot, preferred_element_type=F32)
    accum[...] = jnp.zeros((OWN, 256), F32)

    @pl.loop(0, FAR // 2)
    def _(pair):
        total = accum[...]
        for n in range(2):
            k = pair * 2 + n
            values = jnp.concatenate(
                [far_flat[pl.ds(k * OWN * 2 + half, OWN, stride=2), :] for half in range(2)], axis=1
            )
            high, low = split(values)
            total = total + dot(jnp.concatenate([high, high], axis=1), operators[k])
            total = total + dot(low, operators[k, 0:256])
        accum[...] = total

    for h in range(2):
        for t in range(2):
            expanded[t * 128 : t * 128 + 128, h * 128 : h * 128 + 128] = accum[
                h * 128 : h * 128 + 128, t * 128 : t * 128 + 128
            ].T

    ones = (lax.broadcasted_iota(jnp.int32, (8, 128), 0) == group).astype(BF16)
    across = (((1,), (1,)), ((), ()))
    for s in range(8):
        high, low = split(near_sums[s * OWN : s * OWN + OWN, :])
        both = lax.dot_general(ones, high, across, preferred_element_type=F32) + lax.dot_general(
            ones, low, across, preferred_element_type=F32
        )
        for g in range(4):
            out[g * 8 + s : g * 8 + s + 1, :] = both[g : g + 1, :]

    for h in range(2):
        lanes = slice(h * 128, h * 128 + 128)
        fx, fy, fz = (factors_of(bodies[d * 32 : d * 32 + 32, lanes]) for d in range(3))
        wide = lambda row: jnp.broadcast_to(expanded[row : row + 1, lanes], (NB, 128))
        total = out[:, lanes]
        for a in range(ORDER):
            for b in range(ORDER):
                inner = wide(a * 36 + b * 6) * fz[0]
                for c in range(1, ORDER):
                    inner = inner + wide(a * 36 + b * 6 + c) * fz[c]
                second = inner * fy[b] if b == 0 else second + inner * fy[b]
            total = total + second * fx[a]
        mine = own_first + h * 128 + lax.broadcasted_iota(jnp.int32, (1, 128), 1)
        itself = (near_list[:, lanes] == mine).astype(F32)
        count = jnp.sum(itself, axis=0, keepdims=True)
        out[:, lanes] = total - (4.0 * count) * bodies[96:128, lanes]

    for step in (1, 2, 3):
        row_copy(step).wait_send()
    beside_copy(0, left).wait_send()
    beside_copy(1, right).wait_send()
    wait_all(outgoing, PLANE - 1, plane_send)
    wait_all(recv, LINE - 1, line_send)


def potential_call(pos, charge, near_list, far_list, slots, m2l):
    vmem = pl.BlockSpec(memory_space=pltpu.VMEM)
    dma = pltpu.SemaphoreType.DMA
    return pl.pallas_call(
        potential_kernel,
        out_shape=jax.ShapeDtypeStruct((NB, OWN), F32),
        in_specs=[pl.BlockSpec(memory_space=pl.ANY)] * 6,
        out_specs=vmem,
        scratch_shapes=[
            pltpu.VMEM((128, OWN), F32),
            pltpu.VMEM((NEAR, OWN), jnp.int32),
            pltpu.VMEM((FAR, OWN), jnp.int32),
            pltpu.SMEM((CAP, PEERS), jnp.int32),
            pltpu.VMEM((OWN, 128), F32),
            pltpu.VMEM((PLANE, LINE, CAP_FAR, 1, 128), F32),
            pltpu.VMEM((PLANE, LINE, CAP_FAR, 1, 128), F32),
            pltpu.VMEM((2, CAP, 128), F32),
            pltpu.VMEM((TABLE, 128), F32),
            pltpu.VMEM((LINE, PLANE, CAP_FAR, 1, 128), F32),
            pltpu.VMEM((2, CAP, 128), F32),
            pltpu.VMEM((NODES, NODES * FAR), F32),
            pltpu.VMEM((NEAR, 1, OWN), jnp.int32),
            pltpu.VMEM((FAR, 1, OWN), jnp.int32),
            pltpu.SMEM((NEAR * OWN,), jnp.int32),
            pltpu.SMEM((FAR * OWN,), jnp.int32),
            pltpu.VMEM((2, 128, 128), F32),
            pltpu.VMEM((2, 256, 128), F32),
            pltpu.VMEM((TABLE * 8, 128), F32),
            pltpu.VMEM((8 * OWN, 128), F32),
            pltpu.VMEM((FAR, OWN // 8, 16, 128), F32),
            pltpu.VMEM((2, 256 * FAR, 128), F32),
            pltpu.VMEM((FAR, 512, 256), BF16),
            pltpu.VMEM((OWN, 256), F32),
            pltpu.VMEM((256, OWN), F32),
            dma((6,)),
            dma((NEAR + FAR,)),
            dma((3,)),
            dma((3,)),
            dma,
            dma,
            dma,
            dma,
            dma((2,)),
            dma((2,)),
        ],
        compiler_params=pltpu.CompilerParams(
            collective_id=0, has_side_effects=True, vmem_limit_bytes=60 * 2**20
        ),
    )(pos, charge, near_list, far_list, slots, m2l)


def per_device(positions, charges, m2l_ops, near_list, far_list, send_slots):
    pos = positions.reshape(3 * NB, OWN)
    return potential_call(pos, charges, near_list.T, far_list.T, send_slots[0].T, m2l_ops)


def solution(mesh):
    in_specs = (
        P(None, None, ("leaf", "sub")),
        P(None, ("leaf", "sub")),
        P(),
        P(("leaf", "sub"), None),
        P(("leaf", "sub"), None),
        P(("leaf", "sub"), None, None),
    )
    out_specs = P(None, ("leaf", "sub"))
    return jax.shard_map(
        per_device, mesh=mesh, in_specs=in_specs, out_specs=out_specs, check_vma=False
    )
```
